128 devices in a mesh: row: 16 (over y, x), col: 2 (over core), depth: 4 (over z).
Axes of the slice: x: 4, y: 4, z: 4, core: 2. Of those that a mesh axis runs over, the one named last changes fastest.
Arguments:
- tokens: bfloat16 [2048, 4096], P('depth', ('col', 'row')), may hold values from -6 to 6
- w_gate: bfloat16 [4096, 14336], P('col', 'row'), may hold values from -0.09375 to 0.09375
- w_up: bfloat16 [4096, 14336], P('col', 'row'), may hold values from -0.09375 to 0.09375
- w_down: bfloat16 [14336, 4096], P('row', 'col'), may hold values from -0.046875 to 0.046875
- d_out: bfloat16 [2048, 4096], P('depth', ('col', 'row')), may hold values from -1.5 to 1.5
Outputs:
- output: bfloat16 [2048, 4096], P('depth', ('col', 'row'))
- d_tokens: bfloat16 [2048, 4096], P('depth', ('col', 'row'))
- grad_gate: bfloat16 [4096, 14336], P(('col', 'depth'), 'row')
- grad_up: bfloat16 [4096, 14336], P(('col', 'depth'), 'row')
- grad_down: bfloat16 [14336, 4096], P(('row', 'depth'), 'col')
The draws below stay inside these ranges and needn't reach their ends.
All inputs are finite; a program needn't handle non-finite values.
Results may differ from the reference program's by a relative error of at most 0.025.
Values may be sent and summed in bfloat16 or wider, within the bound.
No kernel may reach another device: no remote copies, remote signals or barrier semaphores. Data moves between devices by JAX's collectives and lax.ppermute only.
A program may use at most 128 MiB of HBM per device.

```python
import jax
import jax.numpy as jnp
from jax import lax

D = 4096
FF = 14336
TOK_GRP = 512
TOKENS = 2048
N_DEPTH = 4


def levels(key, dims, pieces, least, top_value):
    factor_of = 1.0
    for position, shards_of in pieces:
        draws = jax.random.uniform(jax.random.fold_in(jax.random.fold_in(key, 6), position), (shards_of,), jnp.float32, least / len(pieces), top_value / len(pieces))
        factor_of = factor_of * jnp.repeat(jnp.exp(draws), dims[position] // shards_of).reshape((-1,) + (1,) * (len(dims) - 1 - position))
    return factor_of


def centred(own_key, extent, deviation, bound, pieces=(), held_as=jnp.bfloat16):
    entries = jax.random.normal(own_key, extent, jnp.float32) * deviation
    if len(pieces) > 0:
        entries = levels(own_key, extent, pieces, -0.22, 0.18) * entries
    return jnp.clip(entries, min=-bound, max=bound).astype(held_as)


def setup_inputs(seed: int = 0) -> dict:
    key_list = jax.random.split(jax.random.key(seed), 6)
    tokens = centred(key_list[0], (TOKENS, D), 1.0, 6.0, ((0, 4), (1, 32)))
    w_gate = centred(key_list[1], (D, FF), D ** -0.5, 0.09375, ((0, 2), (1, 16)))
    w_up = centred(key_list[2], (D, FF), D ** -0.5, 0.09375, ((0, 2), (1, 16)))
    w_down = centred(key_list[3], (FF, D), FF ** -0.5, 0.046875, ((0, 16), (1, 2)))
    d_out = centred(key_list[4], (TOKENS, D), 0.25, 1.5, ((0, 4), (1, 32)))
    return dict(tokens=tokens, w_gate=w_gate, w_up=w_up, w_down=w_down, d_out=d_out)


def partial_grad(left, right):
    term = jnp.dot(left.T, right, preferred_element_type=jnp.float32).astype(jnp.bfloat16)
    return lax.optimization_barrier(term).astype(jnp.float32)

def reference(tokens, w_gate, w_up, w_down, d_out):
    gate = jnp.dot(tokens, w_gate, preferred_element_type=jnp.float32)
    up = jnp.dot(tokens, w_up, preferred_element_type=jnp.float32)
    sigmoid_gate = jax.nn.sigmoid(gate)
    act = (gate * sigmoid_gate * up).astype(jnp.bfloat16)
    output = jnp.dot(act, w_down, preferred_element_type=jnp.float32).astype(jnp.bfloat16)
    d_act = jnp.dot(d_out, w_down.T, preferred_element_type=jnp.float32)
    d_gate = (d_act * up * sigmoid_gate * (1.0 + gate * (1.0 - sigmoid_gate))).astype(jnp.bfloat16)
    d_up = (d_act * gate * sigmoid_gate).astype(jnp.bfloat16)
    d_tokens = (jnp.dot(d_gate, w_gate.T, preferred_element_type=jnp.float32) + jnp.dot(d_up, w_up.T, preferred_element_type=jnp.float32)).astype(jnp.bfloat16)
    sum_gate = jnp.zeros((D, FF), jnp.float32)
    sum_up = jnp.zeros((D, FF), jnp.float32)
    sum_down = jnp.zeros((FF, D), jnp.float32)
    for group in range(N_DEPTH):
        lower = group * TOK_GRP
        upper = lower + TOK_GRP
        sum_gate = sum_gate + partial_grad(tokens[lower:upper], d_gate[lower:upper])
        sum_up = sum_up + partial_grad(tokens[lower:upper], d_up[lower:upper])
        sum_down = sum_down + partial_grad(act[lower:upper], d_out[lower:upper])
    return (output, d_tokens, sum_gate.astype(jnp.bfloat16), sum_up.astype(jnp.bfloat16), sum_down.astype(jnp.bfloat16))
```

```python
import functools

import jax
import jax.numpy as jnp
from jax import lax
from jax.experimental import pallas as pl
from jax.experimental.pallas import tpu as pltpu
from jax.sharding import PartitionSpec as P

BF = jnp.bfloat16
F32 = jnp.float32
G = 4
MIB = 1024 * 1024


def here():
    row = lax.axis_index("row")
    return row // G, row % G, lax.axis_index("col"), lax.axis_index("depth")


def ring(pos, core):
    step = 1 - 2 * core
    return [pos, (pos - step + G) % G, (pos + step + G) % G, (pos + 2) % G]


def targets(pos, core):
    own, back, ahead, far = ring(pos, core)
    return [own, ahead, back, far]


def row_shift(kind, array, axis):
    pairs = []
    for y in range(G):
        for x in range(G):
            for core in range(2):
                step = {1: 1 - 2 * core, 2: 2 * core - 1, 3: 2}[kind]
                to_y = (y + step) % G if axis == "y" else y
                to_x = (x + step) % G if axis == "x" else x
                pairs.append(((y * G + x) * 2 + core, (to_y * G + to_x) * 2 + core))
    return lax.ppermute(array, ("row", "col"), pairs)


def depth_shift(kind, array):
    pairs = []
    for core in range(2):
        for z in range(G):
            step = {1: 1 - 2 * core, 2: 2 * core - 1}[kind]
            pairs.append((core * G + z, core * G + (z + step) % G))
    return lax.ppermute(array, ("col", "depth"), pairs)


def swap(array):
    return lax.ppermute(array, "col", [(0, 1), (1, 0)])


def transpose_groups(array):
    pairs = []
    for y in range(G):
        for x in range(G):
            for z in range(G):
                pairs.append(((y * G + x) * G + z, (z * G + x) * G + y))
    return lax.ppermute(array, ("row", "depth"), pairs)


def after(array, *others):
    return lax.optimization_barrier((array,) + others)[0]


def call(body, outs, n_in, scratch, flops, nbytes, out_space=pl.ANY, in_space=pl.ANY):
    return pl.pallas_call(
        body,
        out_shape=outs,
        in_specs=[pl.BlockSpec(memory_space=in_space)] * n_in,
        out_specs=jax.tree.map(lambda _: pl.BlockSpec(memory_space=out_space), outs),
        scratch_shapes=scratch,
        compiler_params=pltpu.CompilerParams(vmem_limit_bytes=48 * MIB),
        cost_estimate=pl.CostEstimate(flops=flops, bytes_accessed=nbytes, transcendentals=0),
    )


def shape(dims, dtype=BF):
    return jax.ShapeDtypeStruct(dims, dtype)


def start_all(copies):
    for item in copies:
        item.start()


def wait_all(copies):
    for item in copies:
        item.wait()


def place_body(axis, *refs):
    ins, out, sems = refs[:G], refs[G], refs[G + 1]
    y, x, core, _ = here()
    spots = ring(y if axis == "y" else x, core)
    copies = [pltpu.make_async_copy(ins[k], out.at[spots[k]], sems.at[k]) for k in range(G)]
    start_all(copies)
    wait_all(copies)


def place(axis, parts):
    tok, feat = parts[0].shape
    return call(
        functools.partial(place_body, axis),
        shape((G, tok, feat)),
        G,
        [pltpu.SemaphoreType.DMA((G,))],
        0,
        G * tok * feat * 4,
    )(*parts)


def wide(ref, chunk):
    return jnp.concatenate([ref[chunk, j] for j in range(G)], axis=1)


def split_rows(core, acc, keep, send, half):
    keep[...] = acc[pl.ds(pl.multiple_of(core * half, half), half), :]
    send[...] = acc[pl.ds(pl.multiple_of((1 - core) * half, half), half), :].astype(BF)


def gate_up_body(t0, t1, t2, t3, wg, wu, keep, send, tok, wgs, wus, acc_g, acc_u, sems):
    y, _, core, _ = here()
    spots = ring(y, core)
    loads = [
        pltpu.make_async_copy(ref, tok.at[spots[k]], sems.at[k])
        for k, ref in enumerate((t0, t1, t2, t3))
    ]
    depth = wg.shape[0] // G
    weights = []
    for k in range(G):
        rows = pl.ds(k * depth, depth)
        weights.append(
            [
                pltpu.make_async_copy(wg.at[rows], wgs.at[rows], sems.at[G + 2 * k]),
                pltpu.make_async_copy(wu.at[rows], wus.at[rows], sems.at[G + 2 * k + 1]),
            ]
        )
    start_all(loads)
    for pair in weights:
        start_all(pair)
    wait_all(loads)
    for k in range(G):
        wait_all(weights[k])
        left = wide(tok, k)
        rows = slice(k * depth, (k + 1) * depth)
        for acc, ws in ((acc_g, wgs), (acc_u, wus)):
            term = jnp.dot(left, ws[rows, :], preferred_element_type=F32)
            if k == 0:
                acc[...] = term
            else:
                acc[...] += term
    half = acc_g.shape[0] // 2
    split_rows(core, acc_g, keep.at[0], send.at[0], half)
    split_rows(core, acc_u, keep.at[1], send.at[1], half)


def gate_up(chunks, wg, wu):
    tok = chunks[0].shape[1]
    feats, hid = wg.shape
    return call(
        gate_up_body,
        (shape((2, tok // 2, hid), F32), shape((2, tok // 2, hid))),
        6,
        [
            pltpu.VMEM((G,) + chunks[0].shape, BF),
            pltpu.VMEM((feats, hid), BF),
            pltpu.VMEM((feats, hid), BF),
            pltpu.VMEM((tok, hid), F32),
            pltpu.VMEM((tok, hid), F32),
            pltpu.SemaphoreType.DMA((3 * G,)),
        ],
        4 * tok * feats * hid,
        4 * feats * hid,
        out_space=pltpu.VMEM,
    )(*chunks, wg, wu)


def d_act_body(c0, c1, c2, c3, wd, keep, send, rows_out, cot, wds, acc, flat, sems):
    _, x, core, _ = here()
    spots = ring(x, core)
    loads = [
        pltpu.make_async_copy(ref, cot.at[:, spots[k]], sems.at[k])
        for k, ref in enumerate((c0, c1, c2, c3))
    ]
    depth = wd.shape[1] // G
    weights = [
        pltpu.make_async_copy(
            wd.at[:, pl.ds(k * depth, depth)], wds.at[:, pl.ds(k * depth, depth)], sems.at[G + k]
        )
        for k in range(G)
    ]
    start_all(loads)
    start_all(weights)
    wait_all(loads)
    for k in range(G):
        weights[k].wait()
        left = wide(cot, k)
        cols = slice(k * depth, (k + 1) * depth)
        flat[:, cols] = left
        term = lax.dot_general(
            left, wds[:, cols], (((1,), (1,)), ((), ())), preferred_element_type=F32
        )
        if k == 0:
            acc[...] = term
        else:
            acc[...] += term
    out = pltpu.make_async_copy(flat, rows_out, sems.at[2 * G])
    out.start()
    split_rows(core, acc, keep, send, acc.shape[0] // 2)
    out.wait()


def d_act(chunks, wd):
    tok = chunks[0].shape[1]
    hid, feats = wd.shape
    outs = (shape((tok // 2, hid), F32), shape((tok // 2, hid)), shape((tok, feats)))
    vm, anyw = pl.BlockSpec(memory_space=pltpu.VMEM), pl.BlockSpec(memory_space=pl.ANY)
    return pl.pallas_call(
        d_act_body,
        out_shape=outs,
        in_specs=[anyw] * 5,
        out_specs=(vm, vm, anyw),
        scratch_shapes=[
            pltpu.VMEM((G, G) + chunks[0].shape[1:], BF),
            pltpu.VMEM((hid, feats), BF),
            pltpu.VMEM((tok, hid), F32),
            pltpu.VMEM((tok, feats), BF),
            pltpu.SemaphoreType.DMA((2 * G + 1,)),
        ],
        compiler_params=pltpu.CompilerParams(vmem_limit_bytes=48 * MIB),
        cost_estimate=pl.CostEstimate(
            flops=2 * tok * feats * hid, bytes_accessed=2 * feats * hid, transcendentals=0
        ),
    )(*chunks, wd)


def hidden_body(keep, recv, keep_d, recv_d, act, grads):
    gate = keep[0] + recv[0].astype(F32)
    up = keep[1] + recv[1].astype(F32)
    da = keep_d[...] + recv_d[...].astype(F32)
    sig = 1.0 / (1.0 + jnp.exp(-gate))
    silu = gate * sig
    act[...] = (silu * up).astype(BF)
    grads[0] = (da * up * sig * (1.0 + gate * (1.0 - sig))).astype(BF)
    grads[1] = (da * silu).astype(BF)


def hidden(keep, recv, keep_d, recv_d):
    _, half, hid = keep.shape
    tile = half // 4
    three = pl.BlockSpec((2, tile, hid), lambda i: (0, i, 0))
    two = pl.BlockSpec((tile, hid), lambda i: (i, 0))
    return pl.pallas_call(
        hidden_body,
        grid=(4,),
        out_shape=(shape((half, hid)), shape((2, half, hid))),
        in_specs=[three, three, two, two],
        out_specs=(two, three),
        cost_estimate=pl.CostEstimate(
            flops=20 * half * hid, bytes_accessed=24 * half * hid, transcendentals=half * hid
        ),
    )(keep, recv, keep_d, recv_d)


def out_body(own, other, wd, o0, o1, o2, o3, act, wds, res, sems):
    y, _, core, _ = here()
    half = own.shape[0]
    loads = [
        pltpu.make_async_copy(own, act.at[pl.ds(core * half, half)], sems.at[0]),
        pltpu.make_async_copy(other, act.at[pl.ds((1 - core) * half, half)], sems.at[1]),
    ]
    width = wd.shape[1] // G
    weights = [
        pltpu.make_async_copy(
            wd.at[:, pl.ds(k * width, width)], wds.at[:, pl.ds(k * width, width)], sems.at[2 + k]
        )
        for k in range(G)
    ]
    start_all(loads)
    start_all(weights)
    wait_all(loads)
    part = width // G
    for k in range(G):
        weights[k].wait()
        term = jnp.dot(
            act[...], wds[:, k * width : (k + 1) * width], preferred_element_type=F32
        ).astype(BF)
        for j in range(G):
            res[k, j] = term[:, j * part : (j + 1) * part]
    spots = targets(y, core)
    stores = [
        pltpu.make_async_copy(res.at[spots[k]], ref, sems.at[2 + G + k])
        for k, ref in enumerate((o0, o1, o2, o3))
    ]
    start_all(stores)
    wait_all(stores)


def out_parts(own, other, wd):
    half, hid = own.shape
    feats = wd.shape[1]
    tok = 2 * half
    part = feats // (G * G)
    return call(
        out_body,
        (shape((G, tok, part)),) * G,
        3,
        [
            pltpu.VMEM((tok, hid), BF),
            pltpu.VMEM((hid, feats), BF),
            pltpu.VMEM((G, G, tok, part), BF),
            pltpu.SemaphoreType.DMA((2 + 2 * G,)),
        ],
        2 * tok * feats * hid,
        2 * feats * hid,
    )(own, other, wd)


def d_tok_body(own, other, wg, wu, o0, o1, o2, o3, grads, wgs, wus, res, sems):
    _, x, core, _ = here()
    half = own.shape[1]
    loads = [
        pltpu.make_async_copy(own, grads.at[:, pl.ds(core * half, half)], sems.at[0]),
        pltpu.make_async_copy(other, grads.at[:, pl.ds((1 - core) * half, half)], sems.at[1]),
    ]
    width = wg.shape[0] // G
    weights = []
    for k in range(G):
        rows = pl.ds(k * width, width)
        weights.append(
            [
                pltpu.make_async_copy(wg.at[rows], wgs.at[rows], sems.at[2 + 2 * k]),
                pltpu.make_async_copy(wu.at[rows], wus.at[rows], sems.at[3 + 2 * k]),
            ]
        )
    start_all(loads)
    for pair in weights:
        start_all(pair)
    wait_all(loads)
    part = width // G
    dims = (((1,), (1,)), ((), ()))
    for k in range(G):
        wait_all(weights[k])
        rows = slice(k * width, (k + 1) * width)
        term = lax.dot_general(grads[0], wgs[rows, :], dims, preferred_element_type=F32)
        term += lax.dot_general(grads[1], wus[rows, :], dims, preferred_element_type=F32)
        term = term.astype(BF)
        for j in range(G):
            res[j, k] = term[:, j * part : (j + 1) * part]
    spots = targets(x, core)
    stores = [
        pltpu.make_async_copy(res.at[spots[k]], ref, sems.at[2 + 2 * G + k])
        for k, ref in enumerate((o0, o1, o2, o3))
    ]
    start_all(stores)
    wait_all(stores)


def d_tok_parts(own, other, wg, wu):
    _, half, hid = own.shape
    feats = wg.shape[0]
    tok = 2 * half
    part = feats // (G * G)
    return call(
        d_tok_body,
        (shape((G, tok, part)),) * G,
        4,
        [
            pltpu.VMEM((2, tok, hid), BF),
            pltpu.VMEM((feats, hid), BF),
            pltpu.VMEM((feats, hid), BF),
            pltpu.VMEM((G, G, tok, part), BF),
            pltpu.SemaphoreType.DMA((2 + 3 * G,)),
        ],
        4 * tok * feats * hid,
        4 * feats * hid,
    )(own, other, wg, wu)


def down_body(own, other, cot, b0, b1, b2, b3, act, cots, res, sems):
    _, _, core, z = here()
    half = own.shape[0]
    loads = [
        pltpu.make_async_copy(own, act.at[pl.ds(core * half, half)], sems.at[0]),
        pltpu.make_async_copy(other, act.at[pl.ds((1 - core) * half, half)], sems.at[1]),
    ]
    width = cot.shape[1] // G
    rights = [
        pltpu.make_async_copy(
            cot.at[:, pl.ds(k * width, width)], cots.at[:, pl.ds(k * width, width)], sems.at[2 + k]
        )
        for k in range(G)
    ]
    start_all(loads)
    start_all(rights)
    wait_all(loads)
    left = act[...].T
    block = res.shape[1]
    for k in range(G):
        rights[k].wait()
        cols = slice(k * width, (k + 1) * width)
        term = jnp.dot(left, cots[:, cols], preferred_element_type=F32).astype(BF)
        for j in range(G):
            res[j, :, cols] = term[j * block : (j + 1) * block, :]
    spots = targets(z, core)
    stores = [
        pltpu.make_async_copy(res.at[spots[k]], ref, sems.at[2 + G + k])
        for k, ref in enumerate((b0, b1, b2, b3))
    ]
    start_all(stores)
    wait_all(stores)


def down_parts(own, other, cot):
    half, hid = own.shape
    tok, feats = cot.shape
    return call(
        down_body,
        (shape((hid // G, feats)),) * G,
        3,
        [
            pltpu.VMEM((tok, hid), BF),
            pltpu.VMEM((tok, feats), BF),
            pltpu.VMEM((G, hid // G, feats), BF),
            pltpu.SemaphoreType.DMA((2 + 2 * G,)),
        ],
        2 * tok * feats * hid,
        2 * tok * feats,
    )(own, other, cot)


def grads_body(tok, p0, p1, p2, p3, p4, p5, p6, p7, gg, gu, toks, lefts, rights, sems):
    _, _, core, z = here()
    own, back, ahead, far = ring(z, core)
    half = p0.shape[1]
    feats = gg.shape[0]
    spots = [
        (own, core), (own, 1 - core),
        (back, core), (ahead, 1 - core),
        (back, 1 - core), (ahead, core),
        (far, core), (far, 1 - core),
    ]
    pieces = (p0, p1, p2, p3, p4, p5, p6, p7)
    load = pltpu.make_async_copy(tok, toks, sems.at[8])
    load.start()
    moves = []
    for k, (group, side) in enumerate(spots):
        moves.append(
            pltpu.make_async_copy(
                pieces[k],
                rights.at[:, pl.ds(pl.multiple_of(group * 2 * half + side * half, half), half)],
                sems.at[k],
            )
        )
    start_all(moves)
    load.wait()
    for group in range(G):
        lefts[:, group * 2 * half : (group + 1) * 2 * half] = toks[
            :, group * feats : (group + 1) * feats
        ].T
    wait_all(moves)
    rows = feats // 2
    for n, out in enumerate((gg, gu)):
        for r in range(2):
            cut = slice(r * rows, (r + 1) * rows)
            out[cut, :] = jnp.dot(
                lefts[cut, :], rights[n], preferred_element_type=F32
            ).astype(BF)


def weight_grads(tok, pieces):
    _, half, hid = pieces[0].shape
    feats = tok.shape[1] // G
    return call(
        grads_body,
        (shape((feats, hid)),) * 2,
        9,
        [
            pltpu.VMEM(tok.shape, BF),
            pltpu.VMEM((feats, 2 * G * half), BF),
            pltpu.VMEM((2, 2 * G * half, hid), BF),
            pltpu.SemaphoreType.DMA((9,)),
        ],
        8 * G * half * feats * hid,
        20 * half * hid,
        out_space=pltpu.VMEM,
    )(tok, *pieces)


def mid_sum_body(axis, a0, a1, a2, a3, o0, o1, o2, o3):
    y, x, core, _ = here()
    spots = targets(y if axis == "y" else x, core)
    for k, out in enumerate((o0, o1, o2, o3)):
        at = spots[k]
        total = a0[at].astype(F32) + a1[at].astype(F32) + (a2[at].astype(F32) + a3[at].astype(F32))
        out[...] = total.astype(BF)


def mid_sum(axis, parts):
    _, tok, part = parts[0].shape
    return call(
        functools.partial(mid_sum_body, axis),
        (shape((tok, part)),) * G,
        G,
        [],
        12 * tok * part,
        40 * tok * part,
        out_space=pltpu.VMEM,
        in_space=pltpu.VMEM,
    )(*parts)


def total_of(parts):
    total = parts[0].astype(F32)
    for item in parts[1:]:
        total = total + item.astype(F32)
    return total.astype(BF)


def gather_axis(first, array):
    return [array] + [row_shift(k, array, first) for k in (1, 2, 3)]


def local(tokens, w_gate, w_up, w_down, d_out):
    chunk_t = place("x", gather_axis("x", tokens))
    chunk_c = place("y", gather_axis("y", d_out))
    tok_chunks = gather_axis("y", chunk_t)
    cot_chunks = gather_axis("x", chunk_c)

    keep_gu, send_gu = gate_up(tok_chunks, w_gate, w_up)
    recv_gu = swap(send_gu)
    keep_d, send_d, cot_rows = d_act(cot_chunks, w_down)
    recv_d = swap(send_d)

    turned = after(transpose_groups(tokens), cot_chunks[1])
    turned_rows = lax.all_gather(turned, "row", axis=1, tiled=True)

    act_own, grads_own = hidden(keep_gu, recv_gu, keep_d, recv_d)
    act_other, grads_other = swap(act_own), swap(grads_own)

    near_own = depth_shift(1, grads_own)
    near_other = depth_shift(1, grads_other)
    far_own = depth_shift(1, near_own)

    outs = out_parts(act_own, act_other, w_down)
    out_got = [outs[0]] + [row_shift(k, outs[k], "y") for k in (1, 2, 3)]
    toks = d_tok_parts(grads_own, grads_other, w_gate, w_up)
    tok_got = [toks[0]] + [row_shift(k, toks[k], "x") for k in (1, 2, 3)]

    blocks = down_parts(act_own, act_other, cot_rows)
    relay = depth_shift(1, after(blocks[3], near_own, near_other))
    back = depth_shift(2, after(blocks[2], relay))
    ahead = depth_shift(1, total_of([blocks[1], relay]))

    out_mid = mid_sum("x", out_got)
    tok_mid = mid_sum("y", tok_got)
    output = total_of([out_mid[0]] + [row_shift(k, out_mid[k], "x") for k in (1, 2, 3)])
    d_tokens = total_of([tok_mid[0]] + [row_shift(k, tok_mid[k], "y") for k in (1, 2, 3)])

    pieces = [
        grads_own, grads_other,
        near_own, swap(near_own),
        near_other, swap(near_other),
        far_own, swap(far_own),
    ]
    grad_gate, grad_up = weight_grads(turned_rows, pieces)
    grad_down = total_of([blocks[0], ahead, back])
    return output, d_tokens, grad_gate, grad_up, grad_down


def solution(mesh):
    placed = (
        P("depth", ("col", "row")),
        P("col", "row"),
        P("col", "row"),
        P("row", "col"),
        P("depth", ("col", "row")),
    )
    return jax.shard_map(
        local,
        mesh=mesh,
        in_specs=placed,
        out_specs=(
            P("depth", ("col", "row")),
            P("depth", ("col", "row")),
            P(("col", "depth"), "row"),
            P(("col", "depth"), "row"),
            P(("row", "depth"), "col"),
        ),
        check_vma=False,
    )
```

```python
import functools

import jax
import jax.numpy as jnp
from jax import lax
from jax.experimental import pallas as pl
from jax.experimental.pallas import tpu as pltpu
from jax.sharding import PartitionSpec as P

BF = jnp.bfloat16
F32 = jnp.float32
G = 4
MIB = 1024 * 1024
VM = pltpu.VMEM
HB = pltpu.HBM


def here():
    row = lax.axis_index("row")
    return row // G, row % G, lax.axis_index("col"), lax.axis_index("depth")


def plane_spots(phase, outgoing):
    y, x, core, _ = here()
    pos = jnp.where(core == phase, x, y)
    ahead, back, far = (pos + 1) % G, (pos + G - 1) % G, (pos + 2) % G
    return [pos, ahead, back, far] if outgoing else [pos, back, ahead, far]


def plane_at(core, k, j):
    return jnp.where(core == 0, k, j), jnp.where(core == 0, j, k)


def ring(pos, core):
    step = 1 - 2 * core
    return [pos, (pos - step + G) % G, (pos + step + G) % G, (pos + 2) % G]


def targets(pos, core):
    own, back, ahead, far = ring(pos, core)
    return [own, ahead, back, far]


def plane_shift(kind, array, phase):
    step = {1: 1, 2: G - 1, 3: 2}[kind]
    pairs = []
    for y in range(G):
        for x in range(G):
            for core in range(2):
                along_x = (core == 0) == (phase == 0)
                to_y = y if along_x else (y + step) % G
                to_x = (x + step) % G if along_x else x
                pairs.append(((y * G + x) * 2 + core, (to_y * G + to_x) * 2 + core))
    return lax.ppermute(array, ("row", "col"), pairs)


def depth_shift(kind, array):
    pairs = []
    for core in range(2):
        for z in range(G):
            step = {1: 1 - 2 * core, 2: 2 * core - 1, 3: 2}[kind]
            pairs.append((core * G + z, core * G + (z + step) % G))
    return lax.ppermute(array, ("col", "depth"), pairs)


def swap(array):
    return lax.ppermute(array, "col", [(0, 1), (1, 0)])


def after(array, *others):
    return lax.optimization_barrier((array,) + others)[0]


def spec(space):
    return pl.BlockSpec(memory_space=space)


def keep_out(array):
    return pltpu.with_memory_space_constraint(array, HB)


COST = 50


def call(body, outs, ins, scratch, flops, nbytes, out_spaces=None, limit=24):
    if out_spaces is None:
        out_spaces = (pl.ANY,) * len(outs)
    return pl.pallas_call(
        body,
        out_shape=outs,
        in_specs=[spec(space) for space in ins],
        out_specs=tuple(spec(space) for space in out_spaces),
        scratch_shapes=scratch,
        compiler_params=pltpu.CompilerParams(vmem_limit_bytes=limit * MIB),
        cost_estimate=pl.CostEstimate(
            flops=flops // COST, bytes_accessed=nbytes // COST, transcendentals=0
        ),
    )


def shape(dims, dtype=BF):
    return jax.ShapeDtypeStruct(dims, dtype)


def start_all(copies):
    for item in copies:
        item.start()


def wait_all(copies):
    for item in copies:
        item.wait()


def place_body(p0, p1, p2, p3, tok, cot):
    spots = plane_spots(0, False)
    for k, ref in enumerate((p0, p1, p2, p3)):
        tok[spots[k]] = ref[0]
        cot[spots[k]] = ref[1]


def place(parts):
    _, tok, feat = parts[0].shape
    return call(
        place_body,
        (shape((G, tok, feat)), shape((G, tok, feat))),
        (VM,) * G,
        [],
        0,
        G * tok * feat * 8,
        (VM, VM),
    )(*parts)


def pick_body(c0, c1, c2, c3, o0, o1, o2, o3, tok, sems, out_sems):
    _, _, core, z = here()
    spots = plane_spots(1, False)
    loads = [
        pltpu.make_async_copy(ref, tok.at[spots[k]], sems.at[k])
        for k, ref in enumerate((c0, c1, c2, c3))
    ]
    start_all(loads)
    groups = targets(z, core)
    stores = [
        pltpu.make_async_copy(
            tok.at[plane_at(core, groups[k], j)], ref.at[j], out_sems.at[k, j]
        )
        for k, ref in enumerate((o0, o1, o2, o3))
        for j in range(G)
    ]
    wait_all(loads)
    start_all(stores)
    wait_all(stores)


def pick(chunks):
    _, tok, part = chunks[0].shape
    return call(
        pick_body,
        (shape((G, tok, part)),) * G,
        (pl.ANY,) * G,
        [
            pltpu.VMEM((G, G, tok, part), BF),
            pltpu.SemaphoreType.DMA((G,)),
            pltpu.SemaphoreType.DMA((G, G)),
        ],
        0,
        4 * G * G * tok * part,
        limit=16,
    )(*chunks)


def wide(core, ref, chunk):
    return jnp.concatenate([ref[plane_at(core, chunk, j)] for j in range(G)], axis=1)


def keep_rows(core, acc, keep, sem):
    half = keep.shape[0]
    return pltpu.make_async_copy(
        acc.at[pl.ds(pl.multiple_of(core * half, half), half), :], keep, sem
    )


def send_rows(core, acc, stage, send, sem):
    half = send.shape[0]
    stage[...] = acc[pl.ds(pl.multiple_of((1 - core) * half, half), half), :].astype(BF)
    return pltpu.make_async_copy(stage, send, sem)


def gate_up_body(t0, t1, t2, t3, wg, wu, keep, send, tok, wgs, wus, acc_g, acc_u, stage, sems):
    core = lax.axis_index("col")
    spots = plane_spots(1, False)
    loads = [
        pltpu.make_async_copy(ref, tok.at[spots[k]], sems.at[k])
        for k, ref in enumerate((t0, t1, t2, t3))
    ]
    depth = wg.shape[0] // G
    weights = []
    for k in range(G):
        rows = pl.ds(k * depth, depth)
        weights.append(
            [
                pltpu.make_async_copy(wg.at[rows], wgs.at[rows], sems.at[G + 2 * k]),
                pltpu.make_async_copy(wu.at[rows], wus.at[rows], sems.at[G + 2 * k + 1]),
            ]
        )
    start_all(loads)
    for pair in weights:
        start_all(pair)
    wait_all(loads)
    for k in range(G):
        wait_all(weights[k])
        left = wide(core, tok, k)
        rows = slice(k * depth, (k + 1) * depth)
        for acc, ws in ((acc_g, wgs), (acc_u, wus)):
            term = jnp.dot(left, ws[rows, :], preferred_element_type=F32)
            if k == 0:
                acc[...] = term
            else:
                acc[...] += term
    kept = [
        keep_rows(core, acc_g, keep.at[0], sems.at[0]),
        keep_rows(core, acc_u, keep.at[1], sems.at[1]),
    ]
    start_all(kept)
    for n, acc in enumerate((acc_g, acc_u)):
        sent = send_rows(core, acc, stage.at[n], send.at[n], sems.at[2 + n])
        sent.start()
        kept.append(sent)
    wait_all(kept)


def gate_up(chunks, wg, wu):
    tok = chunks[0].shape[1]
    feats, hid = wg.shape
    return call(
        gate_up_body,
        (shape((2, tok // 2, hid), F32), shape((2, tok // 2, hid))),
        (pl.ANY,) * G + (HB, HB),
        [
            pltpu.VMEM((G,) + chunks[0].shape, BF),
            pltpu.VMEM((feats, hid), BF),
            pltpu.VMEM((feats, hid), BF),
            pltpu.VMEM((tok, hid), F32),
            pltpu.VMEM((tok, hid), F32),
            pltpu.VMEM((2, tok // 2, hid), BF),
            pltpu.SemaphoreType.DMA((3 * G,)),
        ],
        4 * tok * feats * hid,
        4 * feats * hid,
        (HB, pl.ANY),
    )(*chunks, keep_out(wg), keep_out(wu))


def d_act_body(c0, c1, c2, c3, wd, keep, send, cot, wds, acc, stage, sems):
    core = lax.axis_index("col")
    spots = plane_spots(1, False)
    loads = [
        pltpu.make_async_copy(ref, cot.at[spots[k]], sems.at[k])
        for k, ref in enumerate((c0, c1, c2, c3))
    ]
    depth = wd.shape[1] // G
    weights = [
        pltpu.make_async_copy(
            wd.at[:, pl.ds(k * depth, depth)], wds.at[:, pl.ds(k * depth, depth)], sems.at[G + k]
        )
        for k in range(G)
    ]
    start_all(weights)
    start_all(loads)
    wait_all(loads)
    for k in range(G):
        weights[k].wait()
        left = wide(core, cot, k)
        cols = slice(k * depth, (k + 1) * depth)
        term = lax.dot_general(
            left, wds[:, cols], (((1,), (1,)), ((), ())), preferred_element_type=F32
        )
        if k == 0:
            acc[...] = term
        else:
            acc[...] += term
    kept = keep_rows(core, acc, keep, sems.at[0])
    kept.start()
    sent = send_rows(core, acc, stage, send, sems.at[1])
    sent.start()
    kept.wait()
    sent.wait()


def d_act(chunks, wd):
    tok = chunks[0].shape[1]
    hid, feats = wd.shape
    return call(
        d_act_body,
        (shape((tok // 2, hid), F32), shape((tok // 2, hid))),
        (pl.ANY,) * G + (HB,),
        [
            pltpu.VMEM((G,) + chunks[0].shape, BF),
            pltpu.VMEM((hid, feats), BF),
            pltpu.VMEM((tok, hid), F32),
            pltpu.VMEM((tok // 2, hid), BF),
            pltpu.SemaphoreType.DMA((2 * G,)),
        ],
        2 * tok * feats * hid,
        2 * feats * hid,
        (HB, pl.ANY),
    )(*chunks, keep_out(wd))


TILES = 4


def hidden_body(keep, recv, keep_d, recv_d, shares, grads, ks, rs, kds, rds, res, sems):
    tile = keep_d.shape[0] // TILES
    loads, stores = [], []
    for t in range(TILES):
        at = pl.ds(t * tile, tile)
        loads.append(
            [
                pltpu.make_async_copy(keep.at[:, at], ks.at[:, at], sems.at[t, 0]),
                pltpu.make_async_copy(recv.at[:, at], rs.at[:, at], sems.at[t, 1]),
                pltpu.make_async_copy(keep_d.at[at], kds.at[at], sems.at[t, 2]),
                pltpu.make_async_copy(recv_d.at[at], rds.at[at], sems.at[t, 3]),
            ]
        )
        stores.append(
            [
                pltpu.make_async_copy(res.at[:, at], shares.at[:, at], sems.at[t, 4]),
                pltpu.make_async_copy(res.at[pl.ds(1, 2), at], grads.at[:, at], sems.at[t, 5]),
            ]
        )
    for item in loads:
        start_all(item)
    for t in range(TILES):
        wait_all(loads[t])

        @pl.loop(0, tile // 16)
        def _(i):
            rows = pl.ds(pl.multiple_of(t * tile + i * 16, 16), 16)
            gate = ks[0, rows, :] + rs[0, rows, :].astype(F32)
            up = ks[1, rows, :] + rs[1, rows, :].astype(F32)
            da = kds[rows, :] + rds[rows, :].astype(F32)
            sig = 1.0 / (1.0 + jnp.exp(-gate))
            silu = gate * sig
            res[0, rows, :] = (silu * up).astype(BF)
            res[1, rows, :] = (da * up * sig * (1.0 + gate * (1.0 - sig))).astype(BF)
            res[2, rows, :] = (da * silu).astype(BF)

        start_all(stores[t])
    for item in stores:
        wait_all(item)


def hidden(keep, recv, keep_d, recv_d):
    _, half, hid = keep.shape
    return call(
        hidden_body,
        (shape((3, half, hid)), shape((2, half, hid))),
        (HB,) * 4,
        [
            pltpu.VMEM((2, half, hid), F32),
            pltpu.VMEM((2, half, hid), BF),
            pltpu.VMEM((half, hid), F32),
            pltpu.VMEM((half, hid), BF),
            pltpu.VMEM((3, half, hid), BF),
            pltpu.SemaphoreType.DMA((TILES, 6)),
        ],
        20 * half * hid,
        24 * half * hid,
    )(keep_out(keep), keep_out(recv), keep_out(keep_d), keep_out(recv_d))


def out_body(own, other, wd, o0, o1, o2, o3, copied, act, wds, res, held, sems):
    core = lax.axis_index("col")
    half = own.shape[1]
    loads = [
        pltpu.make_async_copy(own.at[0], act.at[pl.ds(core * half, half)], sems.at[0]),
        pltpu.make_async_copy(other.at[0], act.at[pl.ds((1 - core) * half, half)], sems.at[1]),
    ]
    moved = [
        pltpu.make_async_copy(other.at[pl.ds(1, 2)], held, sems.at[2 + 2 * G]),
        pltpu.make_async_copy(held, copied, sems.at[3 + 2 * G]),
    ]
    width = wd.shape[1] // G
    weights = [
        pltpu.make_async_copy(
            wd.at[:, pl.ds(k * width, width)], wds.at[:, pl.ds(k * width, width)], sems.at[2 + k]
        )
        for k in range(G)
    ]
    start_all(loads)
    start_all(weights)
    moved[0].start()
    wait_all(loads)
    part = width // G
    for k in range(G):
        weights[k].wait()
        term = jnp.dot(
            act[...], wds[:, k * width : (k + 1) * width], preferred_element_type=F32
        ).astype(BF)
        for j in range(G):
            res[plane_at(core, k, j)] = term[:, j * part : (j + 1) * part]
    moved[0].wait()
    moved[1].start()
    spots = plane_spots(1, True)
    stores = [
        pltpu.make_async_copy(res.at[spots[k]], ref, sems.at[2 + G + k])
        for k, ref in enumerate((o0, o1, o2, o3))
    ]
    start_all(stores)
    wait_all(stores)
    moved[1].wait()


def out_parts(own, other, wd):
    _, half, hid = own.shape
    feats = wd.shape[1]
    tok = 2 * half
    part = feats // (G * G)
    return call(
        out_body,
        (shape((G, tok, part)),) * G + (shape((2, half, hid)),),
        (pl.ANY, pl.ANY, HB),
        [
            pltpu.VMEM((tok, hid), BF),
            pltpu.VMEM((hid, feats), BF),
            pltpu.VMEM((G, G, tok, part), BF),
            pltpu.VMEM((2, half, hid), BF),
            pltpu.SemaphoreType.DMA((4 + 2 * G,)),
        ],
        2 * tok * feats * hid,
        2 * feats * hid,
    )(own, other, keep_out(wd))


def d_tok_body(own, other, wg, wu, o0, o1, o2, o3, grads, wgs, wus, res, sems):
    core = lax.axis_index("col")
    half = own.shape[1]
    loads = [
        pltpu.make_async_copy(
            own.at[pl.ds(1, 2)], grads.at[:, pl.ds(core * half, half)], sems.at[0]
        ),
        pltpu.make_async_copy(
            other.at[pl.ds(1, 2)], grads.at[:, pl.ds((1 - core) * half, half)], sems.at[1]
        ),
    ]
    width = wg.shape[0] // G
    weights = []
    for k in range(G):
        rows = pl.ds(k * width, width)
        weights.append(
            [
                pltpu.make_async_copy(wg.at[rows], wgs.at[rows], sems.at[2 + 2 * k]),
                pltpu.make_async_copy(wu.at[rows], wus.at[rows], sems.at[3 + 2 * k]),
            ]
        )
    start_all(loads)
    for pair in weights:
        start_all(pair)
    wait_all(loads)
    part = width // G
    dims = (((1,), (1,)), ((), ()))
    for k in range(G):
        wait_all(weights[k])
        rows = slice(k * width, (k + 1) * width)
        term = lax.dot_general(grads[0], wgs[rows, :], dims, preferred_element_type=F32)
        term += lax.dot_general(grads[1], wus[rows, :], dims, preferred_element_type=F32)
        term = term.astype(BF)
        for j in range(G):
            res[plane_at(core, k, j)] = term[:, j * part : (j + 1) * part]
    spots = plane_spots(1, True)
    stores = [
        pltpu.make_async_copy(res.at[spots[k]], ref, sems.at[2 + 2 * G + k])
        for k, ref in enumerate((o0, o1, o2, o3))
    ]
    start_all(stores)
    wait_all(stores)


def d_tok_parts(own, other, wg, wu):
    _, half, hid = own.shape
    feats = wg.shape[0]
    tok = 2 * half
    part = feats // (G * G)
    return call(
        d_tok_body,
        (shape((G, tok, part)),) * G,
        (pl.ANY, pl.ANY, HB, HB),
        [
            pltpu.VMEM((2, tok, hid), BF),
            pltpu.VMEM((feats, hid), BF),
            pltpu.VMEM((feats, hid), BF),
            pltpu.VMEM((G, G, tok, part), BF),
            pltpu.SemaphoreType.DMA((2 + 3 * G,)),
        ],
        4 * tok * feats * hid,
        4 * feats * hid,
    )(own, other, keep_out(wg), keep_out(wu))


def down_body(own, other, c0, c1, c2, c3, b0, b1, b2, b3, act, cot, res, sems):
    _, _, core, z = here()
    half = own.shape[1]
    spots = plane_spots(1, False)
    loads = [
        pltpu.make_async_copy(own.at[0], act.at[pl.ds(core * half, half)], sems.at[0]),
        pltpu.make_async_copy(other.at[0], act.at[pl.ds((1 - core) * half, half)], sems.at[1]),
    ]
    rights = [
        pltpu.make_async_copy(ref, cot.at[spots[k]], sems.at[2 + k])
        for k, ref in enumerate((c0, c1, c2, c3))
    ]
    start_all(loads)
    start_all(rights)
    wait_all(loads)
    left = act[...].T
    wait_all(rights)
    block = res.shape[1]
    width = res.shape[2] // G
    for k in range(G):
        cols = slice(k * width, (k + 1) * width)
        term = jnp.dot(left, wide(core, cot, k), preferred_element_type=F32).astype(BF)
        for j in range(G):
            res[j, :, cols] = term[j * block : (j + 1) * block, :]
    spots = targets(z, core)
    stores = [
        pltpu.make_async_copy(res.at[spots[k]], ref, sems.at[2 + G + k])
        for k, ref in enumerate((b0, b1, b2, b3))
    ]
    start_all(stores)
    wait_all(stores)


def down_parts(own, other, chunks):
    _, half, hid = own.shape
    _, tok, part = chunks[0].shape
    feats = G * G * part
    return call(
        down_body,
        (shape((hid // G, feats)),) * G,
        (pl.ANY,) * (2 + G),
        [
            pltpu.VMEM((tok, hid), BF),
            pltpu.VMEM((G,) + chunks[0].shape, BF),
            pltpu.VMEM((G, hid // G, feats), BF),
            pltpu.SemaphoreType.DMA((2 + 2 * G,)),
        ],
        2 * tok * feats * hid,
        2 * tok * feats,
    )(own, other, *chunks)


def grads_body(t0, t1, t2, t3, p0, p1, p2, p3, p4, p5, p6, p7, gg, gu, toks, lefts, rights, sems):
    _, _, core, z = here()
    own, back, ahead, far = ring(z, core)
    half = p0.shape[1]
    feats = gg.shape[0]
    spots = [
        (own, core), (own, 1 - core),
        (back, core), (ahead, 1 - core),
        (back, 1 - core), (ahead, core),
        (far, core), (far, 1 - core),
    ]
    pieces = (p0, p1, p2, p3, p4, p5, p6, p7)
    places = ring(z, core)
    loads = [
        pltpu.make_async_copy(ref, toks.at[places[k]], sems.at[8 + k])
        for k, ref in enumerate((t0, t1, t2, t3))
    ]
    start_all(loads)
    moves = []
    for k, (group, side) in enumerate(spots):
        moves.append(
            pltpu.make_async_copy(
                pieces[k],
                rights.at[:, pl.ds(pl.multiple_of(group * 2 * half + side * half, half), half)],
                sems.at[k],
            )
        )
    start_all(moves)
    wait_all(loads)
    for group in range(G):
        lefts[:, group * 2 * half : (group + 1) * 2 * half] = jnp.concatenate(
            [toks[group, j] for j in range(G)], axis=1
        ).T
    wait_all(moves)
    rows = feats // 2
    for n, out in enumerate((gg, gu)):
        for r in range(2):
            cut = slice(r * rows, (r + 1) * rows)
            out[cut, :] = jnp.dot(
                lefts[cut, :], rights[n], preferred_element_type=F32
            ).astype(BF)


def weight_grads(chunks, pieces):
    _, half, hid = pieces[0].shape
    _, tok, part = chunks[0].shape
    feats = G * part
    return call(
        grads_body,
        (shape((feats, hid)),) * 2,
        (pl.ANY,) * 6 + (HB,) * 6,
        [
            pltpu.VMEM((G, G, tok, part), BF),
            pltpu.VMEM((feats, 2 * G * half), BF),
            pltpu.VMEM((2, 2 * G * half, hid), BF),
            pltpu.SemaphoreType.DMA((12,)),
        ],
        8 * G * half * feats * hid,
        20 * half * hid,
        (VM, VM),
        30,
    )(*chunks, *pieces[:2], *map(keep_out, pieces[2:]))


def mid_sum_body(a0, a1, a2, a3, b0, b1, b2, b3, o0, o1, o2, o3):
    spots = plane_spots(0, True)
    for k, out in enumerate((o0, o1, o2, o3)):
        at = spots[k]
        for n, (p, q, r, s) in enumerate(((a0, a1, a2, a3), (b0, b1, b2, b3))):
            total = p[at].astype(F32) + q[at].astype(F32) + (r[at].astype(F32) + s[at].astype(F32))
            out[n] = total.astype(BF)


def mid_sum(first, second):
    _, tok, part = first[0].shape
    return call(
        mid_sum_body,
        (shape((2, tok, part)),) * G,
        (VM,) * (2 * G),
        [],
        24 * tok * part,
        80 * tok * part,
        (VM,) * G,
    )(*first, *second)


def last_sum_body(p0, p1, p2, p3, out, tok):
    for n, ref in enumerate((out, tok)):
        total = p0[n].astype(F32) + p1[n].astype(F32) + (p2[n].astype(F32) + p3[n].astype(F32))
        ref[...] = total.astype(BF)


def last_sum(parts):
    _, tok, part = parts[0].shape
    return call(
        last_sum_body,
        (shape((tok, part)),) * 2,
        (VM,) * G,
        [],
        8 * tok * part,
        20 * tok * part,
        (VM, VM),
    )(*parts)


def total_body(count, *refs):
    ins, out, slots, res, sems = refs[:count], refs[count], *refs[count + 1 :]
    tile = out.shape[0] // 2
    loads, stores = [], []
    for t in range(2):
        at = pl.ds(t * tile, tile)
        loads.append(
            [
                pltpu.make_async_copy(ref.at[at], slots.at[n, at], sems.at[t, n])
                for n, ref in enumerate(ins)
            ]
        )
        stores.append(pltpu.make_async_copy(res.at[at], out.at[at], sems.at[t, count]))
    for item in loads:
        start_all(item)
    for t in range(2):
        wait_all(loads[t])

        @pl.loop(0, tile // 16)
        def _(i):
            rows = pl.ds(pl.multiple_of(t * tile + i * 16, 16), 16)
            total = slots[0, rows, :].astype(F32)
            for n in range(1, count):
                total = total + slots[n, rows, :].astype(F32)
            res[rows, :] = total.astype(BF)

        stores[t].start()
    wait_all(stores)


def total_of(parts):
    rows, cols = parts[0].shape
    count = len(parts)
    return call(
        functools.partial(total_body, count),
        (shape((rows, cols)),),
        (pl.ANY,) * count,
        [
            pltpu.VMEM((count, rows, cols), BF),
            pltpu.VMEM((rows, cols), BF),
            pltpu.SemaphoreType.DMA((2, count + 1)),
        ],
        count * rows * cols,
        2 * (count + 1) * rows * cols,
    )(*parts)[0]


def plane_gather(phase, array):
    return [array] + [plane_shift(k, array, phase) for k in (1, 2, 3)]


def local(tokens, w_gate, w_up, w_down, d_out):
    first = plane_gather(0, jnp.stack([tokens, d_out]))
    chunk_t, chunk_c = place(first)
    tok_chunks = plane_gather(1, chunk_t)
    cot_chunks = [chunk_c] + [
        plane_shift(k, after(chunk_c, tok_chunks[k]), 1) for k in (1, 2, 3)
    ]
    picked = pick(tok_chunks)
    group1, group2 = depth_shift(1, picked[1]), depth_shift(2, picked[2])

    keep_gu, send_gu = gate_up([after(tok_chunks[0], picked[0])] + tok_chunks[1:], w_gate, w_up)
    keep_d, send_d = d_act(
        [after(cot_chunks[0], keep_gu, group1)] + cot_chunks[1:], w_down
    )
    group3 = depth_shift(3, after(picked[3], group1, group2))
    recv_gu, recv_d = swap(after(send_gu, send_d)), swap(send_d)

    own, grads_own = hidden(keep_gu, recv_gu, keep_d, recv_d)
    other = swap(own)
    near_own = depth_shift(1, after(grads_own, group2))

    *outs, grads_other = out_parts(after(own, group2), other, w_down)
    blocks = down_parts(own, other, [after(cot_chunks[0], outs[0])] + cot_chunks[1:])
    near_other = depth_shift(1, after(grads_other, blocks[0], group3))
    toks = d_tok_parts(after(own, blocks[0], group3), other, w_gate, w_up)

    out_got = [plane_shift(k, outs[k], 1) for k in (1, 2, 3)]
    stage = lax.optimization_barrier((near_own, toks, out_got))
    near_own, toks, out_got = stage
    far_own = depth_shift(1, near_own)
    relay = depth_shift(1, after(blocks[3], near_other))
    tok_got = [plane_shift(k, toks[k], 1) for k in (1, 2, 3)]

    joined = total_of([blocks[1], relay])
    ahead = depth_shift(1, joined)
    back = depth_shift(2, after(blocks[2], far_own))

    middle = mid_sum([after(outs[0], joined, far_own)] + out_got, [toks[0]] + tok_got)
    last = [plane_shift(k, middle[k], 0) for k in (1, 2, 3)]
    swapped = [swap(after(item, far_own)) for item in (near_own, near_other, far_own)]

    pieces = [
        grads_own, grads_other,
        near_own, swapped[0],
        near_other, swapped[1],
        far_own, swapped[2],
    ]
    grad_gate, grad_up = weight_grads([picked[0], group1, group2, group3], pieces)
    output, d_tokens = last_sum([after(middle[0], grad_gate)] + last)
    grad_down = total_of([after(blocks[0], grad_gate), back, ahead])
    return output, d_tokens, grad_gate, grad_up, grad_down


def solution(mesh):
    placed = (
        P("depth", ("col", "row")),
        P("col", "row"),
        P("col", "row"),
        P("row", "col"),
        P("depth", ("col", "row")),
    )
    return jax.shard_map(
        local,
        mesh=mesh,
        in_specs=placed,
        out_specs=(
            P("depth", ("col", "row")),
            P("depth", ("col", "row")),
            P(("col", "depth"), "row"),
            P(("col", "depth"), "row"),
            P(("row", "depth"), "col"),
        ),
        check_vma=False,
    )
```

```python
import functools

import jax
import jax.numpy as jnp
from jax import lax
from jax.experimental import pallas as pl
from jax.experimental.pallas import tpu as pltpu
from jax.sharding import PartitionSpec as P

BF = jnp.bfloat16
F32 = jnp.float32
G = 4
MIB = 1024 * 1024
VM = pltpu.VMEM
HB = pltpu.HBM


def here():
    row = lax.axis_index("row")
    return row // G, row % G, lax.axis_index("col"), lax.axis_index("depth")


def plane_spots(phase, outgoing):
    y, x, core, _ = here()
    pos = jnp.where(core == phase, x, y)
    ahead, back, far = (pos + 1) % G, (pos + G - 1) % G, (pos + 2) % G
    return [pos, ahead, back, far] if outgoing else [pos, back, ahead, far]


def plane_at(core, k, j):
    return jnp.where(core == 0, k, j), jnp.where(core == 0, j, k)


def ring(pos, core):
    step = 1 - 2 * core
    return [pos, (pos - step + G) % G, (pos + step + G) % G, (pos + 2) % G]


def targets(pos, core):
    own, back, ahead, far = ring(pos, core)
    return [own, ahead, back, far]


def plane_shift(kind, array, phase):
    step = {1: 1, 2: G - 1, 3: 2}[kind]
    pairs = []
    for y in range(G):
        for x in range(G):
            for core in range(2):
                along_x = (core == 0) == (phase == 0)
                to_y = y if along_x else (y + step) % G
                to_x = (x + step) % G if along_x else x
                pairs.append(((y * G + x) * 2 + core, (to_y * G + to_x) * 2 + core))
    return lax.ppermute(array, ("row", "col"), pairs)


def depth_shift(kind, array):
    pairs = []
    for core in range(2):
        for z in range(G):
            step = {1: 1 - 2 * core, 2: 2 * core - 1, 3: 2}[kind]
            pairs.append((core * G + z, core * G + (z + step) % G))
    return lax.ppermute(array, ("col", "depth"), pairs)


def swap(array):
    return lax.ppermute(array, "col", [(0, 1), (1, 0)])


def after(array, *others):
    return lax.optimization_barrier((array,) + others)[0]


def spec(space):
    return pl.BlockSpec(memory_space=space)


def keep_out(array):
    return pltpu.with_memory_space_constraint(array, HB)


COST = 50


def call(body, outs, ins, scratch, flops, nbytes, out_spaces=None, limit=24):
    if out_spaces is None:
        out_spaces = (pl.ANY,) * len(outs)
    return pl.pallas_call(
        body,
        out_shape=outs,
        in_specs=[spec(space) for space in ins],
        out_specs=tuple(spec(space) for space in out_spaces),
        scratch_shapes=scratch,
        compiler_params=pltpu.CompilerParams(vmem_limit_bytes=limit * MIB),
        cost_estimate=pl.CostEstimate(
            flops=flops // COST, bytes_accessed=nbytes // COST, transcendentals=0
        ),
    )


def shape(dims, dtype=BF):
    return jax.ShapeDtypeStruct(dims, dtype)


def start_all(copies):
    for item in copies:
        item.start()


def wait_all(copies):
    for item in copies:
        item.wait()


def place_body(p0, p1, p2, p3, tok, cot):
    spots = plane_spots(0, False)
    for k, ref in enumerate((p0, p1, p2, p3)):
        tok[spots[k]] = ref[0]
        cot[spots[k]] = ref[1]


def place(parts):
    _, tok, feat = parts[0].shape
    return call(
        place_body,
        (shape((G, tok, feat)), shape((G, tok, feat))),
        (VM,) * G,
        [],
        0,
        G * tok * feat * 8,
        (VM, VM),
    )(*parts)


def pick_body(c0, c1, c2, c3, o0, o1, o2, o3, sems):
    y, _, core, z = here()
    ins, outs = (c0, c1, c2, c3), (o0, o1, o2, o3)
    gap = (y - z + G) % G
    came, goes = (0, -1, 1, 2), (0, 1, -1, 2)
    for d in range(G):

        @pl.when((core == 0) & (gap == d))
        def _(d=d):
            copies = []
            for m in range(G):
                k = next(k for k in range(G) if (d + came[k] - goes[m]) % G == 0)
                copies.append(pltpu.make_async_copy(ins[k], outs[m], sems.at[m]))
            start_all(copies)
            wait_all(copies)

    @pl.when(core == 1)
    def _():
        spots = plane_spots(1, False)
        groups = targets(z, core)
        copies = [
            pltpu.make_async_copy(ins[k].at[groups[m]], outs[m].at[spots[k]], sems.at[G + m * G + k])
            for m in range(G)
            for k in range(G)
        ]
        start_all(copies)
        wait_all(copies)


def pick(chunks):
    _, tok, part = chunks[0].shape
    return call(
        pick_body,
        (shape((G, tok, part)),) * G,
        (pl.ANY,) * G,
        [pltpu.SemaphoreType.DMA((G + G * G,))],
        0,
        4 * G * G * tok * part,
        limit=16,
    )(*chunks)


def wide(ref):
    return jnp.concatenate([ref[j] for j in range(G)], axis=1)


def feature(core, spot, j, part):
    at = jnp.where(core == 0, spot * G + j, j * G + spot) * part
    return pl.ds(pl.multiple_of(at, part), part)


def slot_loads(source, target, sems, axis):
    core = lax.axis_index("col")
    spots = plane_spots(1, False)
    part = source.shape[axis] // (G * G)
    copies = []
    for k in range(G):
        row = []
        for j in range(G):
            src, dst = feature(core, spots[k], j, part), pl.ds((k * G + j) * part, part)
            if axis == 0:
                pair = source.at[src], target.at[dst]
            else:
                pair = source.at[:, src], target.at[:, dst]
            row.append(pltpu.make_async_copy(*pair, sems.at[k, j]))
        copies.append(row)
    return copies


def in_order(core, own, other):
    first = jnp.where(core == 0, own, other)
    second = jnp.where(core == 0, other, own)
    return jnp.concatenate([first, second], axis=0)


def keep_rows(core, acc, keep, sem):
    half = keep.shape[0]
    return pltpu.make_async_copy(
        acc.at[pl.ds(pl.multiple_of(core * half, half), half), :], keep, sem
    )


def send_rows(core, acc, stage, send, sem):
    half = send.shape[0]
    stage[...] = acc[pl.ds(pl.multiple_of((1 - core) * half, half), half), :].astype(BF)
    return pltpu.make_async_copy(stage, send, sem)


def weights_body(wg, wu, wd, wgs, wus, wds, w_sems):
    loads = [
        slot_loads(wg, wgs, w_sems.at[0], 0),
        slot_loads(wu, wus, w_sems.at[1], 0),
        slot_loads(wd, wds, w_sems.at[2], 1),
    ]
    for item in loads:
        for row in item:
            start_all(row)
    for item in loads:
        for row in item:
            wait_all(row)


def slot_weights(wg, wu, wd):
    return call(
        weights_body,
        (shape(wg.shape), shape(wu.shape), shape(wd.shape)),
        (HB,) * 3,
        [pltpu.SemaphoreType.DMA((3, G, G))],
        0,
        12 * wg.shape[0] * wg.shape[1],
        (VM,) * 3,
        limit=16,
    )(keep_out(wg), keep_out(wu), keep_out(wd))


def gate_up_body(t0, t1, t2, t3, wg, wu, keep, send, acc_g, acc_u, stage, sems):
    core = lax.axis_index("col")
    depth = wg.shape[0] // G
    for k, ref in enumerate((t0, t1, t2, t3)):
        left = wide(ref)
        rows = slice(k * depth, (k + 1) * depth)
        for acc, ws in ((acc_g, wg), (acc_u, wu)):
            term = jnp.dot(left, ws[rows, :], preferred_element_type=F32)
            if k == 0:
                acc[...] = term
            else:
                acc[...] += term
    kept = [
        keep_rows(core, acc_g, keep.at[0], sems.at[0]),
        keep_rows(core, acc_u, keep.at[1], sems.at[1]),
    ]
    start_all(kept)
    for n, acc in enumerate((acc_g, acc_u)):
        sent = send_rows(core, acc, stage.at[n], send.at[n], sems.at[2 + n])
        sent.start()
        kept.append(sent)
    wait_all(kept)


def gate_up(chunks, wg, wu):
    tok = chunks[0].shape[1]
    feats, hid = wg.shape
    return call(
        gate_up_body,
        (shape((2, tok // 2, hid), F32), shape((2, tok // 2, hid))),
        (VM,) * (G + 2),
        [
            pltpu.VMEM((tok, hid), F32),
            pltpu.VMEM((tok, hid), F32),
            pltpu.VMEM((2, tok // 2, hid), BF),
            pltpu.SemaphoreType.DMA((4,)),
        ],
        4 * tok * feats * hid,
        4 * feats * hid,
    )(*chunks, wg, wu)


def d_act_body(c0, c1, c2, c3, wd, earlier, keep, send, acc, sems):
    core = lax.axis_index("col")
    depth = wd.shape[1] // G
    send[:2] = earlier[...]
    for k, ref in enumerate((c0, c1, c2, c3)):
        cols = slice(k * depth, (k + 1) * depth)
        term = lax.dot_general(
            wide(ref), wd[:, cols], (((1,), (1,)), ((), ())), preferred_element_type=F32
        )
        if k == 0:
            acc[...] = term
        else:
            acc[...] += term
    kept = keep_rows(core, acc, keep, sems.at[0])
    kept.start()
    half = send.shape[1]
    send[2] = acc[pl.ds(pl.multiple_of((1 - core) * half, half), half), :].astype(BF)
    kept.wait()


def d_act(chunks, wd, earlier):
    tok = chunks[0].shape[1]
    hid, feats = wd.shape
    return call(
        d_act_body,
        (shape((tok // 2, hid), F32), shape((3, tok // 2, hid))),
        (VM,) * (G + 2),
        [
            pltpu.VMEM((tok, hid), F32),
            pltpu.SemaphoreType.DMA((1,)),
        ],
        2 * tok * feats * hid,
        2 * feats * hid,
        (pl.ANY, VM),
    )(*chunks, wd, earlier)


def hidden_body(keep, keep_d, recv, shares, grads):
    @pl.loop(0, keep_d.shape[0] // 16)
    def _(i):
        rows = pl.ds(pl.multiple_of(i * 16, 16), 16)
        gate = keep[0, rows, :] + recv[0, rows, :].astype(F32)
        up = keep[1, rows, :] + recv[1, rows, :].astype(F32)
        da = keep_d[rows, :] + recv[2, rows, :].astype(F32)
        sig = 1.0 / (1.0 + jnp.exp(-gate))
        silu = gate * sig
        shares[0, rows, :] = (silu * up).astype(BF)
        dg = (da * up * sig * (1.0 + gate * (1.0 - sig))).astype(BF)
        du = (da * silu).astype(BF)
        shares[1, rows, :] = dg
        shares[2, rows, :] = du
        grads[0, rows, :] = dg
        grads[1, rows, :] = du


def hidden(keep, keep_d, recv):
    _, half, hid = keep.shape
    return call(
        hidden_body,
        (shape((3, half, hid)), shape((2, half, hid))),
        (VM,) * 3,
        [],
        20 * half * hid,
        24 * half * hid,
        (VM, VM),
        limit=16,
    )(keep, keep_d, recv)


OUTGOING = (0, 2, 1, 3)


def out_body(own, other, wd, o0, o1, o2, o3, copied, act):
    core = lax.axis_index("col")
    act[...] = in_order(core, own[0], other[0])
    copied[...] = other[1:]
    width = wd.shape[1] // G
    part = width // G
    for k, ref in zip(OUTGOING, (o0, o1, o2, o3)):
        term = jnp.dot(
            act[...], wd[:, k * width : (k + 1) * width], preferred_element_type=F32
        ).astype(BF)
        for j in range(G):
            ref[j] = term[:, j * part : (j + 1) * part]


def out_parts(own, other, wd):
    _, half, hid = own.shape
    feats = wd.shape[1]
    tok = 2 * half
    part = feats // (G * G)
    return call(
        out_body,
        (shape((G, tok, part)),) * G + (shape((2, half, hid)),),
        (VM,) * 3,
        [pltpu.VMEM((tok, hid), BF)],
        2 * tok * feats * hid,
        2 * feats * hid,
        (VM,) * 5,
    )(own, other, wd)


def d_tok_body(own, other, wg, wu, o0, o1, o2, o3, grads):
    core = lax.axis_index("col")
    for n in range(2):
        grads[n] = in_order(core, own[1 + n], other[1 + n])
    width = wg.shape[0] // G
    part = width // G
    dims = (((1,), (1,)), ((), ()))
    for k, ref in zip(OUTGOING, (o0, o1, o2, o3)):
        rows = slice(k * width, (k + 1) * width)
        term = lax.dot_general(grads[0], wg[rows, :], dims, preferred_element_type=F32)
        term += lax.dot_general(grads[1], wu[rows, :], dims, preferred_element_type=F32)
        term = term.astype(BF)
        for j in range(G):
            ref[j] = term[:, j * part : (j + 1) * part]


def d_tok_parts(own, other, wg, wu):
    _, half, hid = own.shape
    feats = wg.shape[0]
    tok = 2 * half
    part = feats // (G * G)
    return call(
        d_tok_body,
        (shape((G, tok, part)),) * G,
        (VM,) * 4,
        [pltpu.VMEM((2, tok, hid), BF)],
        4 * tok * feats * hid,
        4 * feats * hid,
        (VM,) * G,
    )(own, other, wg, wu)


def down_body(own, other, c0, c1, c2, c3, b0, b1, b2, b3, turned):
    _, _, core, z = here()
    turned[...] = in_order(core, own[0], other[0]).T
    block = b0.shape[0]
    groups = targets(z, core)
    left = jnp.concatenate(
        [turned[pl.ds(pl.multiple_of(groups[m] * block, block), block), :] for m in range(G)],
        axis=0,
    )
    spots = plane_spots(1, False)
    part = b0.shape[1] // (G * G)
    for k, ref in enumerate((c0, c1, c2, c3)):
        term = jnp.dot(left, wide(ref), preferred_element_type=F32).astype(BF)
        for j in range(G):
            cols = feature(core, spots[k], j, part)
            for m, out in enumerate((b0, b1, b2, b3)):
                out[:, cols] = term[m * block : (m + 1) * block, j * part : (j + 1) * part]


def down_parts(own, other, chunks):
    _, half, hid = own.shape
    _, tok, part = chunks[0].shape
    feats = G * G * part
    return call(
        down_body,
        (shape((hid // G, feats)),) * G,
        (VM,) * (2 + G),
        [pltpu.VMEM((hid, tok), BF)],
        2 * tok * feats * hid,
        2 * tok * feats,
        (VM,) * G,
    )(own, other, *chunks)


def grads_body(t0, t1, t2, t3, p0, p1, p2, p3, p4, p5, p6, p7, gg, gu, acc_g, acc_u):
    core = lax.axis_index("col")
    groups = ((t0, p0, p1), (t1, p2, p4), (t2, p5, p3), (t3, p6, p7))
    for k, (tok, same, cross) in enumerate(groups):
        left = wide(tok).T
        for n, acc in enumerate((acc_g, acc_u)):
            right = in_order(core, same[n], cross[n])
            term = jnp.dot(left, right, preferred_element_type=F32)
            if k == 0:
                acc[...] = term
            else:
                acc[...] += term
    gg[...] = acc_g[...].astype(BF)
    gu[...] = acc_u[...].astype(BF)


def weight_grads(chunks, pieces):
    _, half, hid = pieces[0].shape
    feats = G * chunks[0].shape[2]
    return call(
        grads_body,
        (shape((feats, hid)),) * 2,
        (VM,) * 12,
        [pltpu.VMEM((feats, hid), F32)] * 2,
        8 * G * half * feats * hid,
        20 * half * hid,
        (VM, VM),
        32,
    )(*chunks, *pieces)


def mid_sum_body(a0, a1, a2, a3, b0, b1, b2, b3, o0, o1, o2, o3):
    spots = plane_spots(0, True)
    for k, out in enumerate((o0, o1, o2, o3)):
        at = spots[k]
        for n, (p, q, r, s) in enumerate(((a0, a1, a2, a3), (b0, b1, b2, b3))):
            total = p[at].astype(F32) + q[at].astype(F32) + (r[at].astype(F32) + s[at].astype(F32))
            out[n] = total.astype(BF)


def mid_sum(first, second):
    _, tok, part = first[0].shape
    return call(
        mid_sum_body,
        (shape((2, tok, part)),) * G,
        (VM,) * (2 * G),
        [],
        24 * tok * part,
        80 * tok * part,
        (VM,) * G,
    )(*first, *second)


def last_sum_body(p0, p1, p2, p3, out, tok):
    for n, ref in enumerate((out, tok)):
        total = p0[n].astype(F32) + p1[n].astype(F32) + (p2[n].astype(F32) + p3[n].astype(F32))
        ref[...] = total.astype(BF)


def last_sum(parts):
    _, tok, part = parts[0].shape
    return call(
        last_sum_body,
        (shape((tok, part)),) * 2,
        (VM,) * G,
        [],
        8 * tok * part,
        20 * tok * part,
        (VM, VM),
    )(*parts)


PARTS = 2


def total_body(count, *refs):
    ins, out, slots, res, sems = refs[:count], refs[count], *refs[count + 1 :]
    tile = out.shape[0] // PARTS
    loads, stores = [], []
    for t in range(PARTS):
        at = pl.ds(t * tile, tile)
        loads.append(
            [
                pltpu.make_async_copy(ref.at[at], slots.at[n, at], sems.at[t, n])
                for n, ref in enumerate(ins)
            ]
        )
        stores.append(pltpu.make_async_copy(res.at[at], out.at[at], sems.at[t, count]))
    for item in loads:
        start_all(item)
    for t in range(PARTS):
        wait_all(loads[t])

        @pl.loop(0, tile // 16)
        def _(i):
            rows = pl.ds(pl.multiple_of(t * tile + i * 16, 16), 16)
            total = slots[0, rows, :].astype(F32)
            for n in range(1, count):
                total = total + slots[n, rows, :].astype(F32)
            res[rows, :] = total.astype(BF)

        stores[t].start()
    wait_all(stores)


def total_of(parts):
    rows, cols = parts[0].shape
    count = len(parts)
    return call(
        functools.partial(total_body, count),
        (shape((rows, cols)),),
        (pl.ANY,) * count,
        [
            pltpu.VMEM((count, rows, cols), BF),
            pltpu.VMEM((rows, cols), BF),
            pltpu.SemaphoreType.DMA((PARTS, count + 1)),
        ],
        count * rows * cols,
        2 * (count + 1) * rows * cols,
    )(*parts)[0]


def plane_gather(phase, array):
    return [array] + [plane_shift(k, array, phase) for k in (1, 2, 3)]


def local(tokens, w_gate, w_up, w_down, d_out):
    first = plane_gather(0, jnp.stack([tokens, d_out]))
    chunk_t, chunk_c = place(first)
    tok_chunks = plane_gather(1, chunk_t)
    cot_chunks = [chunk_c] + [
        plane_shift(k, after(chunk_c, tok_chunks[k]), 1) for k in (1, 2, 3)
    ]
    w_gate, w_up, w_down = slot_weights(w_gate, w_up, w_down)
    picked = pick(tok_chunks)
    group1, group2 = depth_shift(1, picked[1]), depth_shift(2, picked[2])

    keep_gu, send_gu = gate_up([after(tok_chunks[0], picked[0])] + tok_chunks[1:], w_gate, w_up)
    keep_d, send = d_act(
        [after(cot_chunks[0], group1, group2)] + cot_chunks[1:], w_down, send_gu
    )
    group3 = depth_shift(3, after(picked[3], group1, group2))
    own, grads_own = hidden(keep_gu, keep_d, swap(send))
    other = swap(own)
    near_own = depth_shift(1, grads_own)

    *outs, grads_other = out_parts(own, other, w_down)
    near_other = depth_shift(1, after(grads_other, group3))
    blocks = down_parts(own, other, [after(cot_chunks[0], outs[0])] + cot_chunks[1:])
    toks = d_tok_parts(after(own, blocks[0]), other, w_gate, w_up)

    out_got = [plane_shift(k, outs[k], 1) for k in (1, 2, 3)]
    near_own, toks, out_got = lax.optimization_barrier((near_own, toks, out_got))
    far_own = depth_shift(1, near_own)
    relay = depth_shift(1, after(blocks[3], near_own))
    tok_got = [plane_shift(k, toks[k], 1) for k in (1, 2, 3)]

    joined = total_of([after(blocks[1], near_other), relay])
    ahead = depth_shift(1, joined)
    back = depth_shift(2, after(blocks[2], joined))

    middle = mid_sum([after(outs[0], joined)] + out_got, [toks[0]] + tok_got)
    last = [plane_shift(k, middle[k], 0) for k in (1, 2, 3)]
    swapped = [
        swap(after(item, far_own, joined, *tok_got)) for item in (near_own, near_other, far_own)
    ]

    pieces = [
        grads_own, grads_other,
        near_own, swapped[0],
        near_other, swapped[1],
        far_own, swapped[2],
    ]
    grad_gate, grad_up = weight_grads([picked[0], group1, group2, group3], pieces)
    output, d_tokens = last_sum([after(middle[0], grad_gate)] + last)
    grad_down = total_of([after(blocks[0], grad_gate), back, ahead])
    return output, d_tokens, grad_gate, grad_up, grad_down


def solution(mesh):
    placed = (
        P("depth", ("col", "row")),
        P("col", "row"),
        P("col", "row"),
        P("row", "col"),
        P("depth", ("col", "row")),
    )
    return jax.shard_map(
        local,
        mesh=mesh,
        in_specs=placed,
        out_specs=(
            P("depth", ("col", "row")),
            P("depth", ("col", "row")),
            P(("col", "depth"), "row"),
            P(("col", "depth"), "row"),
            P(("row", "depth"), "col"),
        ),
        check_vma=False,
    )
```

```python
import functools

import jax
import jax.numpy as jnp
from jax import lax
from jax.experimental import pallas as pl
from jax.experimental.pallas import tpu as pltpu
from jax.sharding import PartitionSpec as P

BF = jnp.bfloat16
F32 = jnp.float32
G = 4
MIB = 1024 * 1024
VM = pltpu.VMEM
HB = pltpu.HBM


def here():
    row = lax.axis_index("row")
    return row // G, row % G, lax.axis_index("col"), lax.axis_index("depth")


def plane_spots(phase, outgoing):
    y, x, core, _ = here()
    pos = jnp.where(core == phase, x, y)
    ahead, back, far = (pos + 1) % G, (pos + G - 1) % G, (pos + 2) % G
    return [pos, ahead, back, far] if outgoing else [pos, back, ahead, far]


def plane_at(core, k, j):
    return jnp.where(core == 0, k, j), jnp.where(core == 0, j, k)


def ring(pos, core):
    step = 1 - 2 * core
    return [pos, (pos - step + G) % G, (pos + step + G) % G, (pos + 2) % G]


def targets(pos, core):
    own, back, ahead, far = ring(pos, core)
    return [own, ahead, back, far]


def plane_shift(kind, array, phase):
    step = {1: 1, 2: G - 1, 3: 2}[kind]
    pairs = []
    for y in range(G):
        for x in range(G):
            for core in range(2):
                along_x = (core == 0) == (phase == 0)
                to_y = y if along_x else (y + step) % G
                to_x = (x + step) % G if along_x else x
                pairs.append(((y * G + x) * 2 + core, (to_y * G + to_x) * 2 + core))
    return lax.ppermute(array, ("row", "col"), pairs)


def depth_shift(kind, array):
    pairs = []
    for core in range(2):
        for z in range(G):
            step = {1: 1 - 2 * core, 2: 2 * core - 1, 3: 2}[kind]
            pairs.append((core * G + z, core * G + (z + step) % G))
    return lax.ppermute(array, ("col", "depth"), pairs)


def swap(array):
    return lax.ppermute(array, "col", [(0, 1), (1, 0)])


def after(array, *others):
    return lax.optimization_barrier((array,) + others)[0]


def spec(space):
    return pl.BlockSpec(memory_space=space)


def keep_out(array):
    return pltpu.with_memory_space_constraint(array, HB)


COST = 50


def call(body, outs, ins, scratch, flops, nbytes, out_spaces=None, limit=24):
    if out_spaces is None:
        out_spaces = (pl.ANY,) * len(outs)
    return pl.pallas_call(
        body,
        out_shape=outs,
        in_specs=[spec(space) for space in ins],
        out_specs=tuple(spec(space) for space in out_spaces),
        scratch_shapes=scratch,
        compiler_params=pltpu.CompilerParams(vmem_limit_bytes=limit * MIB),
        cost_estimate=pl.CostEstimate(
            flops=flops // COST, bytes_accessed=nbytes // COST, transcendentals=0
        ),
    )


def shape(dims, dtype=BF):
    return jax.ShapeDtypeStruct(dims, dtype)


def start_all(copies):
    for item in copies:
        item.start()


def wait_all(copies):
    for item in copies:
        item.wait()


def place_body(p0, p1, p2, p3, tok, cot):
    spots = plane_spots(0, False)
    for k, ref in enumerate((p0, p1, p2, p3)):
        tok[spots[k]] = ref[0]
        cot[spots[k]] = ref[1]


def place(parts):
    _, tok, feat = parts[0].shape
    return call(
        place_body,
        (shape((G, tok, feat)), shape((G, tok, feat))),
        (VM,) * G,
        [],
        0,
        G * tok * feat * 8,
        (VM, VM),
    )(*parts)


def pick_body(c0, c1, c2, c3, o0, o1, o2, o3, sems):
    y, _, core, z = here()
    ins, outs = (c0, c1, c2, c3), (o0, o1, o2, o3)
    gap = (y - z + G) % G
    came, goes = (0, -1, 1, 2), (0, 1, -1, 2)
    for d in range(G):

        @pl.when((core == 0) & (gap == d))
        def _(d=d):
            copies = []
            for m in range(G):
                k = next(k for k in range(G) if (d + came[k] - goes[m]) % G == 0)
                copies.append(pltpu.make_async_copy(ins[k], outs[m], sems.at[m]))
            start_all(copies)
            wait_all(copies)

    @pl.when(core == 1)
    def _():
        spots = plane_spots(1, False)
        groups = targets(z, core)
        copies = [
            pltpu.make_async_copy(ins[k].at[groups[m]], outs[m].at[spots[k]], sems.at[G + m * G + k])
            for m in range(G)
            for k in range(G)
        ]
        start_all(copies)
        wait_all(copies)


def pick(chunks):
    _, tok, part = chunks[0].shape
    return call(
        pick_body,
        (shape((G, tok, part)),) * G,
        (pl.ANY,) * G,
        [pltpu.SemaphoreType.DMA((G + G * G,))],
        0,
        4 * G * G * tok * part,
        limit=16,
    )(*chunks)


def wide(ref):
    return jnp.concatenate([ref[j] for j in range(G)], axis=1)


def feature(core, spot, j, part):
    at = jnp.where(core == 0, spot * G + j, j * G + spot) * part
    return pl.ds(pl.multiple_of(at, part), part)


def slot_loads(source, target, sems, axis):
    core = lax.axis_index("col")
    spots = plane_spots(1, False)
    part = source.shape[axis] // (G * G)
    copies = []
    for k in range(G):
        row = []
        for j in range(G):
            src, dst = feature(core, spots[k], j, part), pl.ds((k * G + j) * part, part)
            if axis == 0:
                pair = source.at[src], target.at[dst]
            else:
                pair = source.at[:, src], target.at[:, dst]
            row.append(pltpu.make_async_copy(*pair, sems.at[k, j]))
        copies.append(row)
    return copies


def in_order(core, own, other):
    first = jnp.where(core == 0, own, other)
    second = jnp.where(core == 0, other, own)
    return jnp.concatenate([first, second], axis=0)


def keep_rows(core, acc, keep, sem):
    half = keep.shape[0]
    return pltpu.make_async_copy(
        acc.at[pl.ds(pl.multiple_of(core * half, half), half), :], keep, sem
    )


def send_rows(core, acc, stage, send, sem):
    half = send.shape[0]
    stage[...] = acc[pl.ds(pl.multiple_of((1 - core) * half, half), half), :].astype(BF)
    return pltpu.make_async_copy(stage, send, sem)


def weights_body(wg, wu, wd, wgs, wus, wds, w_sems):
    loads = [
        slot_loads(wg, wgs, w_sems.at[0], 0),
        slot_loads(wu, wus, w_sems.at[1], 0),
        slot_loads(wd, wds, w_sems.at[2], 1),
    ]
    for item in loads:
        for row in item:
            start_all(row)
    for item in loads:
        for row in item:
            wait_all(row)


def slot_weights(wg, wu, wd):
    return call(
        weights_body,
        (shape(wg.shape), shape(wu.shape), shape(wd.shape)),
        (HB,) * 3,
        [pltpu.SemaphoreType.DMA((3, G, G))],
        0,
        12 * wg.shape[0] * wg.shape[1],
        (VM,) * 3,
        limit=16,
    )(keep_out(wg), keep_out(wu), keep_out(wd))


def gate_up_body(t0, t1, t2, t3, wg, wu, keep, send, acc_g, acc_u, stage, sems):
    core = lax.axis_index("col")
    depth = wg.shape[0] // G
    for k, ref in enumerate((t0, t1, t2, t3)):
        left = wide(ref)
        rows = slice(k * depth, (k + 1) * depth)
        for acc, ws in ((acc_g, wg), (acc_u, wu)):
            term = jnp.dot(left, ws[rows, :], preferred_element_type=F32)
            if k == 0:
                acc[...] = term
            else:
                acc[...] += term
    kept = [
        keep_rows(core, acc_g, keep.at[0], sems.at[0]),
        keep_rows(core, acc_u, keep.at[1], sems.at[1]),
    ]
    start_all(kept)
    for n, acc in enumerate((acc_g, acc_u)):
        sent = send_rows(core, acc, stage.at[n], send.at[n], sems.at[2 + n])
        sent.start()
        kept.append(sent)
    wait_all(kept)


def gate_up(chunks, wg, wu):
    tok = chunks[0].shape[1]
    feats, hid = wg.shape
    return call(
        gate_up_body,
        (shape((2, tok // 2, hid), F32), shape((2, tok // 2, hid))),
        (VM,) * (G + 2),
        [
            pltpu.VMEM((tok, hid), F32),
            pltpu.VMEM((tok, hid), F32),
            pltpu.VMEM((2, tok // 2, hid), BF),
            pltpu.SemaphoreType.DMA((4,)),
        ],
        4 * tok * feats * hid,
        4 * feats * hid,
    )(*chunks, wg, wu)


def d_act_body(c0, c1, c2, c3, wd, earlier, keep, send, acc, sems):
    core = lax.axis_index("col")
    depth = wd.shape[1] // G
    send[:2] = earlier[...]
    for k, ref in enumerate((c0, c1, c2, c3)):
        cols = slice(k * depth, (k + 1) * depth)
        term = lax.dot_general(
            wide(ref), wd[:, cols], (((1,), (1,)), ((), ())), preferred_element_type=F32
        )
        if k == 0:
            acc[...] = term
        else:
            acc[...] += term
    kept = keep_rows(core, acc, keep, sems.at[0])
    kept.start()
    half = send.shape[1]
    send[2] = acc[pl.ds(pl.multiple_of((1 - core) * half, half), half), :].astype(BF)
    kept.wait()


def d_act(chunks, wd, earlier):
    tok = chunks[0].shape[1]
    hid, feats = wd.shape
    return call(
        d_act_body,
        (shape((tok // 2, hid), F32), shape((3, tok // 2, hid))),
        (VM,) * (G + 2),
        [
            pltpu.VMEM((tok, hid), F32),
            pltpu.SemaphoreType.DMA((1,)),
        ],
        2 * tok * feats * hid,
        2 * feats * hid,
        (pl.ANY, VM),
    )(*chunks, wd, earlier)


def hidden_body(keep, keep_d, recv, shares, grads):
    @pl.loop(0, keep_d.shape[0] // 16)
    def _(i):
        rows = pl.ds(pl.multiple_of(i * 16, 16), 16)
        gate = keep[0, rows, :] + recv[0, rows, :].astype(F32)
        up = keep[1, rows, :] + recv[1, rows, :].astype(F32)
        da = keep_d[rows, :] + recv[2, rows, :].astype(F32)
        sig = 1.0 / (1.0 + jnp.exp(-gate))
        silu = gate * sig
        shares[0, rows, :] = (silu * up).astype(BF)
        dg = (da * up * sig * (1.0 + gate * (1.0 - sig))).astype(BF)
        du = (da * silu).astype(BF)
        shares[1, rows, :] = dg
        shares[2, rows, :] = du
        grads[0, rows, :] = dg
        grads[1, rows, :] = du


def hidden(keep, keep_d, recv):
    _, half, hid = keep.shape
    return call(
        hidden_body,
        (shape((3, half, hid)), shape((2, half, hid))),
        (VM,) * 3,
        [],
        20 * half * hid,
        24 * half * hid,
        (VM, VM),
        limit=16,
    )(keep, keep_d, recv)


OUTGOING = (0, 2, 1, 3)


def out_body(own, other, wd, o0, o1, o2, o3, copied, act):
    core = lax.axis_index("col")
    act[...] = in_order(core, own[0], other[0])
    copied[...] = other[1:]
    width = wd.shape[1] // G
    part = width // G
    for k, ref in zip(OUTGOING, (o0, o1, o2, o3)):
        term = jnp.dot(
            act[...], wd[:, k * width : (k + 1) * width], preferred_element_type=F32
        ).astype(BF)
        for j in range(G):
            ref[j] = term[:, j * part : (j + 1) * part]


def out_parts(own, other, wd):
    _, half, hid = own.shape
    feats = wd.shape[1]
    tok = 2 * half
    part = feats // (G * G)
    return call(
        out_body,
        (shape((G, tok, part)),) * G + (shape((2, half, hid)),),
        (VM,) * 3,
        [pltpu.VMEM((tok, hid), BF)],
        2 * tok * feats * hid,
        2 * feats * hid,
        (VM,) * 5,
    )(own, other, wd)


def d_tok_body(own, other, wg, wu, o0, o1, o2, o3, grads):
    core = lax.axis_index("col")
    for n in range(2):
        grads[n] = in_order(core, own[1 + n], other[1 + n])
    width = wg.shape[0] // G
    part = width // G
    dims = (((1,), (1,)), ((), ()))
    for k, ref in zip(OUTGOING, (o0, o1, o2, o3)):
        rows = slice(k * width, (k + 1) * width)
        term = lax.dot_general(grads[0], wg[rows, :], dims, preferred_element_type=F32)
        term += lax.dot_general(grads[1], wu[rows, :], dims, preferred_element_type=F32)
        term = term.astype(BF)
        for j in range(G):
            ref[j] = term[:, j * part : (j + 1) * part]


def d_tok_parts(own, other, wg, wu):
    _, half, hid = own.shape
    feats = wg.shape[0]
    tok = 2 * half
    part = feats // (G * G)
    return call(
        d_tok_body,
        (shape((G, tok, part)),) * G,
        (VM,) * 4,
        [pltpu.VMEM((2, tok, hid), BF)],
        4 * tok * feats * hid,
        4 * feats * hid,
        (VM,) * G,
    )(own, other, wg, wu)


def down_body(own, other, c0, c1, c2, c3, b0, b1, b2, b3, turned):
    _, _, core, z = here()
    turned[...] = in_order(core, own[0], other[0]).T
    block = b0.shape[0]
    groups = targets(z, core)
    left = jnp.concatenate(
        [turned[pl.ds(pl.multiple_of(groups[m] * block, block), block), :] for m in range(G)],
        axis=0,
    )
    spots = plane_spots(1, False)
    part = b0.shape[1] // (G * G)
    for k, ref in enumerate((c0, c1, c2, c3)):
        term = jnp.dot(left, wide(ref), preferred_element_type=F32).astype(BF)
        for j in range(G):
            cols = feature(core, spots[k], j, part)
            for m, out in enumerate((b0, b1, b2, b3)):
                out[:, cols] = term[m * block : (m + 1) * block, j * part : (j + 1) * part]


def down_parts(own, other, chunks):
    _, half, hid = own.shape
    _, tok, part = chunks[0].shape
    feats = G * G * part
    return call(
        down_body,
        (shape((hid // G, feats)),) * G,
        (VM,) * (2 + G),
        [pltpu.VMEM((hid, tok), BF)],
        2 * tok * feats * hid,
        2 * tok * feats,
        (VM,) * G,
    )(own, other, *chunks)


def grads_body(t0, t1, t2, t3, p0, p1, p2, p3, p4, p5, p6, p7, gg, gu, acc_g, acc_u):
    core = lax.axis_index("col")
    groups = ((t0, p0, p1), (t1, p2, p4), (t2, p5, p3), (t3, p6, p7))
    for k, (tok, same, cross) in enumerate(groups):
        left = wide(tok).T
        for n, acc in enumerate((acc_g, acc_u)):
            right = in_order(core, same[n], cross[n])
            term = jnp.dot(left, right, preferred_element_type=F32)
            if k == 0:
                acc[...] = term
            else:
                acc[...] += term
    gg[...] = acc_g[...].astype(BF)
    gu[...] = acc_u[...].astype(BF)


def weight_grads(chunks, pieces):
    _, half, hid = pieces[0].shape
    feats = G * chunks[0].shape[2]
    return call(
        grads_body,
        (shape((feats, hid)),) * 2,
        (VM,) * 12,
        [pltpu.VMEM((feats, hid), F32)] * 2,
        8 * G * half * feats * hid,
        20 * half * hid,
        (VM, VM),
        32,
    )(*chunks, *pieces)


def mid_sum_body(a0, a1, a2, a3, b0, b1, b2, b3, o0, o1, o2, o3):
    spots = plane_spots(0, True)
    for k, out in enumerate((o0, o1, o2, o3)):
        at = spots[k]
        for n, (p, q, r, s) in enumerate(((a0, a1, a2, a3), (b0, b1, b2, b3))):
            total = p[at].astype(F32) + q[at].astype(F32) + (r[at].astype(F32) + s[at].astype(F32))
            out[n] = total.astype(BF)


def mid_sum(first, second):
    _, tok, part = first[0].shape
    return call(
        mid_sum_body,
        (shape((2, tok, part)),) * G,
        (VM,) * (2 * G),
        [],
        24 * tok * part,
        80 * tok * part,
        (VM,) * G,
    )(*first, *second)


def last_sum_body(p0, p1, p2, p3, out, tok):
    for n, ref in enumerate((out, tok)):
        total = p0[n].astype(F32) + p1[n].astype(F32) + (p2[n].astype(F32) + p3[n].astype(F32))
        ref[...] = total.astype(BF)


def last_sum(parts):
    _, tok, part = parts[0].shape
    return call(
        last_sum_body,
        (shape((tok, part)),) * 2,
        (VM,) * G,
        [],
        8 * tok * part,
        20 * tok * part,
        (VM, VM),
    )(*parts)


def total_body(*refs):
    out = refs[-1]
    rows = 16

    @pl.loop(0, out.shape[0] // rows)
    def _(i):
        at = pl.ds(pl.multiple_of(i * rows, rows), rows)
        total = refs[0][at, :].astype(F32)
        for ref in refs[1:-1]:
            total = total + ref[at, :].astype(F32)
        out[at, :] = total.astype(BF)


def total_of(parts):
    rows, cols = parts[0].shape
    return call(
        total_body,
        (shape((rows, cols)),),
        (VM,) * len(parts),
        [],
        len(parts) * rows * cols,
        2 * (len(parts) + 1) * rows * cols,
        (VM,),
        limit=16,
    )(*parts)[0]


def plane_gather(phase, array):
    return [array] + [plane_shift(k, array, phase) for k in (1, 2, 3)]


def local(tokens, w_gate, w_up, w_down, d_out):
    first = plane_gather(0, jnp.stack([tokens, d_out]))
    chunk_t, chunk_c = place(first)
    tok_chunks = plane_gather(1, chunk_t)
    cot_chunks = [chunk_c] + [
        plane_shift(k, after(chunk_c, tok_chunks[k]), 1) for k in (1, 2, 3)
    ]
    w_gate, w_up, w_down = slot_weights(w_gate, w_up, w_down)
    picked = pick([after(tok_chunks[0], w_gate)] + tok_chunks[1:])
    group1, group3 = depth_shift(1, picked[1]), depth_shift(3, picked[3])

    keep_gu, send_gu = gate_up([after(tok_chunks[0], picked[0])] + tok_chunks[1:], w_gate, w_up)
    keep_d, send = d_act(
        [after(cot_chunks[0], group1, group3)] + cot_chunks[1:], w_down, send_gu
    )
    group2 = depth_shift(2, after(picked[2], group1, group3))
    own, grads_own = hidden(keep_gu, keep_d, swap(send))
    other = swap(own)
    near_own = depth_shift(1, grads_own)

    *outs, grads_other = out_parts(own, other, w_down)
    near_other = depth_shift(1, after(grads_other, group2))
    blocks = down_parts(own, other, [after(cot_chunks[0], outs[0])] + cot_chunks[1:])
    toks = d_tok_parts(after(own, blocks[0]), other, w_gate, w_up)

    out_got = [plane_shift(k, outs[k], 1) for k in (1, 2, 3)]
    near_own, toks, out_got = lax.optimization_barrier((near_own, toks, out_got))
    far_own = depth_shift(1, near_own)
    relay = depth_shift(1, after(blocks[3], near_own))
    tok_got = [plane_shift(k, toks[k], 1) for k in (1, 2, 3)]

    joined = total_of([after(blocks[1], near_other), relay])
    ahead = depth_shift(1, joined)
    back = depth_shift(2, after(blocks[2], joined))

    middle = mid_sum([after(outs[0], joined)] + out_got, [toks[0]] + tok_got)
    last = [plane_shift(k, middle[k], 0) for k in (1, 2, 3)]
    swapped = [
        swap(after(item, far_own, joined, *tok_got)) for item in (near_own, near_other, far_own)
    ]

    pieces = [
        grads_own, grads_other,
        near_own, swapped[0],
        near_other, swapped[1],
        far_own, swapped[2],
    ]
    grad_gate, grad_up = weight_grads([picked[0], group1, group2, group3], pieces)
    output, d_tokens = last_sum([after(middle[0], grad_gate)] + last)
    grad_down = total_of([after(blocks[0], grad_gate), back, ahead])
    return output, d_tokens, grad_gate, grad_up, grad_down


def solution(mesh):
    placed = (
        P("depth", ("col", "row")),
        P("col", "row"),
        P("col", "row"),
        P("row", "col"),
        P("depth", ("col", "row")),
    )
    return jax.shard_map(
        local,
        mesh=mesh,
        in_specs=placed,
        out_specs=(
            P("depth", ("col", "row")),
            P("depth", ("col", "row")),
            P(("col", "depth"), "row"),
            P(("col", "depth"), "row"),
            P(("row", "depth"), "col"),
        ),
        check_vma=False,
    )
```

```python
import functools

import jax
import jax.numpy as jnp
from jax import lax
from jax.experimental import pallas as pl
from jax.experimental.pallas import tpu as pltpu
from jax.sharding import PartitionSpec as P

BF = jnp.bfloat16
F32 = jnp.float32
G = 4
MIB = 1024 * 1024
VM = pltpu.VMEM
HB = pltpu.HBM


def here():
    row = lax.axis_index("row")
    return row // G, row % G, lax.axis_index("col"), lax.axis_index("depth")


def plane_spots(phase, outgoing):
    y, x, core, _ = here()
    pos = jnp.where(core == phase, x, y)
    ahead, back, far = (pos + 1) % G, (pos + G - 1) % G, (pos + 2) % G
    return [pos, ahead, back, far] if outgoing else [pos, back, ahead, far]


def plane_at(core, k, j):
    return jnp.where(core == 0, k, j), jnp.where(core == 0, j, k)


def ring(pos, core):
    step = 1 - 2 * core
    return [pos, (pos - step + G) % G, (pos + step + G) % G, (pos + 2) % G]


def targets(pos, core):
    own, back, ahead, far = ring(pos, core)
    return [own, ahead, back, far]


def plane_shift(kind, array, phase):
    step = {1: 1, 2: G - 1, 3: 2}[kind]
    pairs = []
    for y in range(G):
        for x in range(G):
            for core in range(2):
                along_x = (core == 0) == (phase == 0)
                to_y = y if along_x else (y + step) % G
                to_x = (x + step) % G if along_x else x
                pairs.append(((y * G + x) * 2 + core, (to_y * G + to_x) * 2 + core))
    return lax.ppermute(array, ("row", "col"), pairs)


def depth_shift(kind, array):
    pairs = []
    for core in range(2):
        for z in range(G):
            step = {1: 1 - 2 * core, 2: 2 * core - 1, 3: 2}[kind]
            pairs.append((core * G + z, core * G + (z + step) % G))
    return lax.ppermute(array, ("col", "depth"), pairs)


def swap(array):
    return lax.ppermute(array, "col", [(0, 1), (1, 0)])


def after(array, *others):
    return lax.optimization_barrier((array,) + others)[0]


def spec(space):
    return pl.BlockSpec(memory_space=space)


def keep_out(array):
    return pltpu.with_memory_space_constraint(array, HB)


COST = 50


def call(body, outs, ins, scratch, flops, nbytes, out_spaces=None, limit=24):
    if out_spaces is None:
        out_spaces = (pl.ANY,) * len(outs)
    return pl.pallas_call(
        body,
        out_shape=outs,
        in_specs=[spec(space) for space in ins],
        out_specs=tuple(spec(space) for space in out_spaces),
        scratch_shapes=scratch,
        compiler_params=pltpu.CompilerParams(vmem_limit_bytes=limit * MIB),
        cost_estimate=pl.CostEstimate(
            flops=flops // COST, bytes_accessed=nbytes // COST, transcendentals=0
        ),
    )


def shape(dims, dtype=BF):
    return jax.ShapeDtypeStruct(dims, dtype)


def start_all(copies):
    for item in copies:
        item.start()


def wait_all(copies):
    for item in copies:
        item.wait()


def place_body(p0, p1, p2, p3, tok, cot):
    spots = plane_spots(0, False)
    for k, ref in enumerate((p0, p1, p2, p3)):
        tok[spots[k]] = ref[0]
        cot[spots[k]] = ref[1]


def place(parts):
    _, tok, feat = parts[0].shape
    return call(
        place_body,
        (shape((G, tok, feat)), shape((G, tok, feat))),
        (VM,) * G,
        [],
        0,
        G * tok * feat * 8,
        (VM, VM),
    )(*parts)


def pick_body(c0, c1, c2, c3, o0, o1, o2, o3, sems):
    y, _, core, z = here()
    ins, outs = (c0, c1, c2, c3), (o0, o1, o2, o3)
    gap = (y - z + G) % G
    came, goes = (0, -1, 1, 2), (0, 1, -1, 2)
    for d in range(G):

        @pl.when((core == 0) & (gap == d))
        def _(d=d):
            copies = []
            for m in range(G):
                k = next(k for k in range(G) if (d + came[k] - goes[m]) % G == 0)
                copies.append(pltpu.make_async_copy(ins[k], outs[m], sems.at[m]))
            start_all(copies)
            wait_all(copies)

    @pl.when(core == 1)
    def _():
        spots = plane_spots(1, False)
        groups = targets(z, core)
        copies = [
            pltpu.make_async_copy(ins[k].at[groups[m]], outs[m].at[spots[k]], sems.at[G + m * G + k])
            for m in range(G)
            for k in range(G)
        ]
        start_all(copies)
        wait_all(copies)


def pick(chunks):
    _, tok, part = chunks[0].shape
    return call(
        pick_body,
        (shape((G, tok, part)),) * G,
        (pl.ANY,) * G,
        [pltpu.SemaphoreType.DMA((G + G * G,))],
        0,
        4 * G * G * tok * part,
        limit=16,
    )(*chunks)


def wide(ref):
    return jnp.concatenate([ref[j] for j in range(G)], axis=1)


def feature(core, spot, j, part):
    at = jnp.where(core == 0, spot * G + j, j * G + spot) * part
    return pl.ds(pl.multiple_of(at, part), part)


def slot_loads(source, target, sems, axis):
    core = lax.axis_index("col")
    spots = plane_spots(1, False)
    part = source.shape[axis] // (G * G)
    copies = []
    for k in range(G):
        row = []
        for j in range(G):
            src, dst = feature(core, spots[k], j, part), pl.ds((k * G + j) * part, part)
            if axis == 0:
                pair = source.at[src], target.at[dst]
            else:
                pair = source.at[:, src], target.at[:, dst]
            row.append(pltpu.make_async_copy(*pair, sems.at[k, j]))
        copies.append(row)
    return copies


def in_order(core, own, other):
    first = jnp.where(core == 0, own, other)
    second = jnp.where(core == 0, other, own)
    return jnp.concatenate([first, second], axis=0)


def keep_rows(core, acc, keep, sem):
    half = keep.shape[0]
    return pltpu.make_async_copy(
        acc.at[pl.ds(pl.multiple_of(core * half, half), half), :], keep, sem
    )


def send_rows(core, acc, stage, send, sem):
    half = send.shape[0]
    stage[...] = acc[pl.ds(pl.multiple_of((1 - core) * half, half), half), :].astype(BF)
    return pltpu.make_async_copy(stage, send, sem)


def weights_body(wg, wu, wd, wgs, wus, wds, w_sems):
    loads = [
        slot_loads(wg, wgs, w_sems.at[0], 0),
        slot_loads(wu, wus, w_sems.at[1], 0),
        slot_loads(wd, wds, w_sems.at[2], 1),
    ]
    for item in loads:
        for row in item:
            start_all(row)
    for item in loads:
        for row in item:
            wait_all(row)


def slot_weights(wg, wu, wd):
    return call(
        weights_body,
        (shape(wg.shape), shape(wu.shape), shape(wd.shape)),
        (HB,) * 3,
        [pltpu.SemaphoreType.DMA((3, G, G))],
        0,
        12 * wg.shape[0] * wg.shape[1],
        (VM,) * 3,
        limit=16,
    )(keep_out(wg), keep_out(wu), keep_out(wd))


def gate_up_body(t0, t1, t2, t3, wg, wu, keep, send, acc_g, acc_u, stage, sems):
    core = lax.axis_index("col")
    depth = wg.shape[0] // G
    for k, ref in enumerate((t0, t1, t2, t3)):
        left = wide(ref)
        rows = slice(k * depth, (k + 1) * depth)
        for acc, ws in ((acc_g, wg), (acc_u, wu)):
            term = jnp.dot(left, ws[rows, :], preferred_element_type=F32)
            if k == 0:
                acc[...] = term
            else:
                acc[...] += term
    kept = [
        keep_rows(core, acc_g, keep.at[0], sems.at[0]),
        keep_rows(core, acc_u, keep.at[1], sems.at[1]),
    ]
    start_all(kept)
    for n, acc in enumerate((acc_g, acc_u)):
        sent = send_rows(core, acc, stage.at[n], send.at[n], sems.at[2 + n])
        sent.start()
        kept.append(sent)
    wait_all(kept)


def gate_up(chunks, wg, wu):
    tok = chunks[0].shape[1]
    feats, hid = wg.shape
    return call(
        gate_up_body,
        (shape((2, tok // 2, hid), F32), shape((2, tok // 2, hid))),
        (VM,) * (G + 2),
        [
            pltpu.VMEM((tok, hid), F32),
            pltpu.VMEM((tok, hid), F32),
            pltpu.VMEM((2, tok // 2, hid), BF),
            pltpu.SemaphoreType.DMA((4,)),
        ],
        4 * tok * feats * hid,
        4 * feats * hid,
    )(*chunks, wg, wu)


def d_act_body(c0, c1, c2, c3, wd, earlier, keep, send, acc, sems):
    core = lax.axis_index("col")
    depth = wd.shape[1] // G
    send[:2] = earlier[...]
    for k, ref in enumerate((c0, c1, c2, c3)):
        cols = slice(k * depth, (k + 1) * depth)
        term = lax.dot_general(
            wide(ref), wd[:, cols], (((1,), (1,)), ((), ())), preferred_element_type=F32
        )
        if k == 0:
            acc[...] = term
        else:
            acc[...] += term
    kept = keep_rows(core, acc, keep, sems.at[0])
    kept.start()
    half = send.shape[1]
    send[2] = acc[pl.ds(pl.multiple_of((1 - core) * half, half), half), :].astype(BF)
    kept.wait()


def d_act(chunks, wd, earlier):
    tok = chunks[0].shape[1]
    hid, feats = wd.shape
    return call(
        d_act_body,
        (shape((tok // 2, hid), F32), shape((3, tok // 2, hid))),
        (VM,) * (G + 2),
        [
            pltpu.VMEM((tok, hid), F32),
            pltpu.SemaphoreType.DMA((1,)),
        ],
        2 * tok * feats * hid,
        2 * feats * hid,
        (pl.ANY, VM),
    )(*chunks, wd, earlier)


def hidden_body(keep, keep_d, recv, shares, grads):
    @pl.loop(0, keep_d.shape[0] // 16)
    def _(i):
        rows = pl.ds(pl.multiple_of(i * 16, 16), 16)
        gate = keep[0, rows, :] + recv[0, rows, :].astype(F32)
        up = keep[1, rows, :] + recv[1, rows, :].astype(F32)
        da = keep_d[rows, :] + recv[2, rows, :].astype(F32)
        sig = 1.0 / (1.0 + jnp.exp(-gate))
        silu = gate * sig
        shares[0, rows, :] = (silu * up).astype(BF)
        dg = (da * up * sig * (1.0 + gate * (1.0 - sig))).astype(BF)
        du = (da * silu).astype(BF)
        shares[1, rows, :] = dg
        shares[2, rows, :] = du
        grads[0, rows, :] = dg
        grads[1, rows, :] = du


def hidden(keep, keep_d, recv):
    _, half, hid = keep.shape
    return call(
        hidden_body,
        (shape((3, half, hid)), shape((2, half, hid))),
        (VM,) * 3,
        [],
        20 * half * hid,
        24 * half * hid,
        (VM, VM),
        limit=16,
    )(keep, keep_d, recv)


OUTGOING = (0, 2, 1, 3)


def out_body(own, other, wd, o0, o1, o2, o3, copied, act):
    core = lax.axis_index("col")
    act[...] = in_order(core, own[0], other[0])
    copied[...] = other[1:]
    width = wd.shape[1] // G
    part = width // G
    for k, ref in zip(OUTGOING, (o0, o1, o2, o3)):
        term = jnp.dot(
            act[...], wd[:, k * width : (k + 1) * width], preferred_element_type=F32
        ).astype(BF)
        for j in range(G):
            ref[j] = term[:, j * part : (j + 1) * part]


def out_parts(own, other, wd):
    _, half, hid = own.shape
    feats = wd.shape[1]
    tok = 2 * half
    part = feats // (G * G)
    return call(
        out_body,
        (shape((G, tok, part)),) * G + (shape((2, half, hid)),),
        (VM,) * 3,
        [pltpu.VMEM((tok, hid), BF)],
        2 * tok * feats * hid,
        2 * feats * hid,
        (VM,) * 5,
    )(own, other, wd)


def d_tok_body(own, other, wg, wu, o0, o1, o2, o3, grads):
    core = lax.axis_index("col")
    for n in range(2):
        grads[n] = in_order(core, own[1 + n], other[1 + n])
    width = wg.shape[0] // G
    part = width // G
    dims = (((1,), (1,)), ((), ()))
    for k, ref in zip(OUTGOING, (o0, o1, o2, o3)):
        rows = slice(k * width, (k + 1) * width)
        term = lax.dot_general(grads[0], wg[rows, :], dims, preferred_element_type=F32)
        term += lax.dot_general(grads[1], wu[rows, :], dims, preferred_element_type=F32)
        term = term.astype(BF)
        for j in range(G):
            ref[j] = term[:, j * part : (j + 1) * part]


def d_tok_parts(own, other, wg, wu):
    _, half, hid = own.shape
    feats = wg.shape[0]
    tok = 2 * half
    part = feats // (G * G)
    return call(
        d_tok_body,
        (shape((G, tok, part)),) * G,
        (VM,) * 4,
        [pltpu.VMEM((2, tok, hid), BF)],
        4 * tok * feats * hid,
        4 * feats * hid,
        (VM,) * G,
    )(own, other, wg, wu)


def down_body(own, other, c0, c1, c2, c3, b0, b1, b2, b3, turned):
    _, _, core, z = here()
    turned[...] = in_order(core, own[0], other[0]).T
    block = b0.shape[0]
    groups = targets(z, core)
    left = jnp.concatenate(
        [turned[pl.ds(pl.multiple_of(groups[m] * block, block), block), :] for m in range(G)],
        axis=0,
    )
    spots = plane_spots(1, False)
    part = b0.shape[1] // (G * G)
    for k, ref in enumerate((c0, c1, c2, c3)):
        term = jnp.dot(left, wide(ref), preferred_element_type=F32).astype(BF)
        for j in range(G):
            cols = feature(core, spots[k], j, part)
            for m, out in enumerate((b0, b1, b2, b3)):
                out[:, cols] = term[m * block : (m + 1) * block, j * part : (j + 1) * part]


def down_parts(own, other, chunks):
    _, half, hid = own.shape
    _, tok, part = chunks[0].shape
    feats = G * G * part
    return call(
        down_body,
        (shape((hid // G, feats)),) * G,
        (VM,) * (2 + G),
        [pltpu.VMEM((hid, tok), BF)],
        2 * tok * feats * hid,
        2 * tok * feats,
        (VM,) * G,
    )(own, other, *chunks)


def grads_body(t0, t1, t2, t3, p0, p1, p2, p3, p4, p5, p6, p7, gg, gu, acc_g, acc_u):
    core = lax.axis_index("col")
    groups = ((t0, p0, p1), (t1, p2, p4), (t2, p5, p3), (t3, p6, p7))
    for k, (tok, same, cross) in enumerate(groups):
        left = wide(tok).T
        for n, acc in enumerate((acc_g, acc_u)):
            right = in_order(core, same[n], cross[n])
            term = jnp.dot(left, right, preferred_element_type=F32)
            if k == 0:
                acc[...] = term
            else:
                acc[...] += term
    gg[...] = acc_g[...].astype(BF)
    gu[...] = acc_u[...].astype(BF)


def weight_grads(chunks, pieces):
    _, half, hid = pieces[0].shape
    feats = G * chunks[0].shape[2]
    return call(
        grads_body,
        (shape((feats, hid)),) * 2,
        (VM,) * 12,
        [pltpu.VMEM((feats, hid), F32)] * 2,
        8 * G * half * feats * hid,
        20 * half * hid,
        (VM, VM),
        32,
    )(*chunks, *pieces)


def mid_sum_body(a0, a1, a2, a3, b0, b1, b2, b3, o0, o1, o2, o3):
    spots = plane_spots(0, True)
    for k, out in enumerate((o0, o1, o2, o3)):
        at = spots[k]
        for n, (p, q, r, s) in enumerate(((a0, a1, a2, a3), (b0, b1, b2, b3))):
            total = p[at].astype(F32) + q[at].astype(F32) + (r[at].astype(F32) + s[at].astype(F32))
            out[n] = total.astype(BF)


def mid_sum(first, second):
    _, tok, part = first[0].shape
    return call(
        mid_sum_body,
        (shape((2, tok, part)),) * G,
        (VM,) * (2 * G),
        [],
        24 * tok * part,
        80 * tok * part,
        (VM,) * G,
    )(*first, *second)


def last_sum_body(p0, p1, p2, p3, out, tok):
    for n, ref in enumerate((out, tok)):
        total = p0[n].astype(F32) + p1[n].astype(F32) + (p2[n].astype(F32) + p3[n].astype(F32))
        ref[...] = total.astype(BF)


def last_sum(parts):
    _, tok, part = parts[0].shape
    return call(
        last_sum_body,
        (shape((tok, part)),) * 2,
        (VM,) * G,
        [],
        8 * tok * part,
        20 * tok * part,
        (VM, VM),
    )(*parts)


def total_body(*refs):
    out = refs[-1]
    rows = 16

    @pl.loop(0, out.shape[0] // rows)
    def _(i):
        at = pl.ds(pl.multiple_of(i * rows, rows), rows)
        total = refs[0][at, :].astype(F32)
        for ref in refs[1:-1]:
            total = total + ref[at, :].astype(F32)
        out[at, :] = total.astype(BF)


def total_of(parts):
    rows, cols = parts[0].shape
    return call(
        total_body,
        (shape((rows, cols)),),
        (VM,) * len(parts),
        [],
        len(parts) * rows * cols,
        2 * (len(parts) + 1) * rows * cols,
        (VM,),
        limit=16,
    )(*parts)[0]


def pair_body(first, second, out, sems):
    copies = [
        pltpu.make_async_copy(first, out.at[0], sems.at[0]),
        pltpu.make_async_copy(second, out.at[1], sems.at[1]),
    ]
    start_all(copies)
    wait_all(copies)


def pair(first, second):
    return call(
        pair_body,
        (shape((2,) + first.shape),),
        (HB, HB),
        [pltpu.SemaphoreType.DMA((2,))],
        0,
        8 * first.shape[0] * first.shape[1],
        limit=16,
    )(keep_out(first), keep_out(second))[0]


def plane_gather(phase, array):
    return [array] + [plane_shift(k, array, phase) for k in (1, 2, 3)]


def local(tokens, w_gate, w_up, w_down, d_out):
    first = plane_gather(0, pair(tokens, d_out))
    chunk_t, chunk_c = place(first)
    tok_chunks = plane_gather(1, chunk_t)
    cot_chunks = [chunk_c] + [
        plane_shift(k, after(chunk_c, tok_chunks[k]), 1) for k in (1, 2, 3)
    ]
    w_gate, w_up, w_down = slot_weights(w_gate, w_up, w_down)
    picked = pick([after(tok_chunks[0], w_gate)] + tok_chunks[1:])
    group1, group3 = depth_shift(1, picked[1]), depth_shift(3, picked[3])

    keep_gu, send_gu = gate_up([after(tok_chunks[0], picked[0])] + tok_chunks[1:], w_gate, w_up)
    keep_d, send = d_act(
        [after(cot_chunks[0], group1, group3)] + cot_chunks[1:], w_down, send_gu
    )
    group2 = depth_shift(2, after(picked[2], group1, group3))
    own, grads_own = hidden(keep_gu, keep_d, swap(send))
    other = swap(own)
    near_own = depth_shift(1, grads_own)

    *outs, grads_other = out_parts(own, other, w_down)
    near_other = depth_shift(1, after(grads_other, group2))
    blocks = down_parts(own, other, [after(cot_chunks[0], outs[0])] + cot_chunks[1:])
    toks = d_tok_parts(after(own, blocks[0]), other, w_gate, w_up)

    out_got = [plane_shift(k, outs[k], 1) for k in (1, 2, 3)]
    near_own, toks, out_got = lax.optimization_barrier((near_own, toks, out_got))
    far_own = depth_shift(1, near_own)
    relay = depth_shift(1, after(blocks[3], near_own))
    tok_got = [plane_shift(k, toks[k], 1) for k in (1, 2, 3)]

    joined = total_of([after(blocks[1], near_other), relay])
    ahead = depth_shift(1, joined)
    back = depth_shift(2, after(blocks[2], joined))

    middle = mid_sum([after(outs[0], joined)] + out_got, [toks[0]] + tok_got)
    last = [plane_shift(k, middle[k], 0) for k in (1, 2, 3)]
    swapped = [
        swap(after(item, far_own, joined, *tok_got)) for item in (near_own, near_other, far_own)
    ]

    pieces = [
        grads_own, grads_other,
        near_own, swapped[0],
        near_other, swapped[1],
        far_own, swapped[2],
    ]
    grad_gate, grad_up = weight_grads([picked[0], group1, group2, group3], pieces)
    output, d_tokens = last_sum([after(middle[0], grad_gate)] + last)
    grad_down = total_of([after(blocks[0], grad_gate), back, ahead])
    return output, d_tokens, grad_gate, grad_up, grad_down


def solution(mesh):
    placed = (
        P("depth", ("col", "row")),
        P("col", "row"),
        P("col", "row"),
        P("row", "col"),
        P("depth", ("col", "row")),
    )
    return jax.shard_map(
        local,
        mesh=mesh,
        in_specs=placed,
        out_specs=(
            P("depth", ("col", "row")),
            P("depth", ("col", "row")),
            P(("col", "depth"), "row"),
            P(("col", "depth"), "row"),
            P(("row", "depth"), "col"),
        ),
        check_vma=False,
    )
```
